256 devices in a mesh: genome: 128 (over y_lo, x, z, core), chan: 2 (over y_hi).
Axes of the slice: x: 4, y: 4 (y_hi: 2, y_lo: 2; y = y_hi * 2 + y_lo), z: 8, core: 2. Of those that a mesh axis runs over, the one named last changes fastest.
Arguments:
- embeddings: bfloat16 [4096, 512], P('genome'), may hold values from -6 to 6
- bin_mask: int32 [4096], P('genome'), may hold values 0 or 1
- target: float32 [4096, 256], P('genome'), may hold values from -6 to 6
- proj_weight: bfloat16 [512, 64], P(None, 'chan'), may hold values from -0.25 to 0.25
- dist_bias: bfloat16 [64, 256], P('chan'), may hold values from -3 to 3
- pair_kernel: bfloat16 [9, 64, 64], P(None, 'chan'), may hold values from -0.25 to 0.25
- head_kernel: bfloat16 [9, 64], P(None, 'chan'), may hold values from -0.25 to 0.25
- dilations: int32 [2], replicated, may hold values from 1 to 4, as said below
Outputs:
- emb_grad: float32 [4096, 512], P('genome', 'chan')
- proj_grad: float32 [512, 64], P(None, 'chan')
- pair_grad: float32 [9, 64, 64], P(None, 'chan')
- head_grad: float32 [9, 64], P(None, 'chan')
The draws below stay inside these ranges and needn't reach their ends.
Inputs may be any that keep to these rules, and one draw needn't show every extreme that they name: `dilations`: one of the two rates is 4.
All inputs are finite; a program needn't handle non-finite values. No bound on the sum of `bin_mask` on one device may be relied on, other than what follows from the above.
Results may differ from the reference program's by a relative error of at most 0.0075.
Values may be sent and summed in bfloat16 or wider, within the bound.
No kernel may reach another device: no remote copies, remote signals or barrier semaphores. Data moves between devices by JAX's collectives and lax.ppermute only.
A program may use at most 64 MiB of HBM per device.

```python
import jax
import jax.numpy as jnp
from jax import lax

EMB = 512
CH = 64
BAND = 256
MAXDIL = 4
BINS = 4096


def draw_dilations(key, part):
    key = jax.random.fold_in(key, 11)
    first_key, second_key = jax.random.split(key)
    other_rate = jax.random.randint(first_key, (1,), 1, MAXDIL + 1)
    flipped = jax.random.randint(second_key, (1,), 0, 2)
    top_rate = jnp.full((1,), MAXDIL, jnp.int32)
    leading = jnp.where(flipped == 0, top_rate, other_rate)
    trailing = jnp.where(flipped == 0, other_rate, top_rate)
    return jnp.concatenate([leading, trailing]).astype(jnp.int32)


def plant(drawn, own_key, smallest, largest):
    place = [jax.random.randint(jax.random.fold_in(own_key, axis), (), 0, length) for axis, length in enumerate(drawn.shape)]
    longest = drawn.shape.index(max(drawn.shape))
    neighbour = place[:longest] + [(place[longest] + 1) % drawn.shape[longest]] + place[longest + 1:]
    return drawn.at[tuple(place)].set(smallest).at[tuple(neighbour)].set(largest)


def block_scale(own_key, shape, cuts, low, high):
    def one(axis_at, blocks):
        steps = jax.random.uniform(jax.random.fold_in(jax.random.fold_in(own_key, 6), axis_at), (blocks,), jnp.float32, low / len(cuts), high / len(cuts))
        return jnp.repeat(jnp.exp(steps), shape[axis_at] // blocks).reshape((-1,) + (1,) * (len(shape) - axis_at - 1))

    gain = one(*cuts[0])
    for cut in cuts[1:]:
        gain = gain * one(*cut)
    return gain


def normal_values(rng, dims, scale, limit, cuts=(), kind=jnp.bfloat16):
    result = scale * jax.random.normal(rng, dims, jnp.float32)
    if cuts:
        result = result * block_scale(rng, dims, cuts, -0.22, 0.18)
    return jnp.clip(result, -limit, limit).astype(kind)


def setup_inputs(seed: int = 0) -> dict:
    streams_of = jax.random.split(jax.random.key(seed), 9)
    return {
        "embeddings": normal_values(streams_of[0], (BINS, EMB), 1.0, 6.0, ((0, 128),)),
        "bin_mask": plant((jax.random.randint(streams_of[1], (BINS,), 0, 8) < 7).astype(jnp.int32), jax.random.fold_in(streams_of[1], 1), 0, 1),
        "target": normal_values(streams_of[2], (BINS, BAND), 1.0, 6.0, ((0, 128),), jnp.float32),
        "proj_weight": normal_values(streams_of[3], (EMB, CH), EMB ** -0.5, 0.25, ((1, 2),)),
        "dist_bias": normal_values(streams_of[4], (CH, BAND), 0.5, 3.0, ((0, 2),)),
        "pair_kernel": normal_values(streams_of[5], (9, CH, CH), (9 * CH) ** -0.5, 0.25, ((1, 2),)),
        "head_kernel": normal_values(streams_of[6], (9, CH), (9 * CH) ** -0.5, 0.25, ((1, 2),)),
        "dilations": draw_dilations(jax.random.fold_in(streams_of[8], 71), 0),
    }


row_block = 64
tap_pairs = ((-1, -1), (-1, 0), (-1, 1), (0, -1), (0, 0), (0, 1), (1, -1), (1, 0), (1, 1))


def silu_slope(values):
    sigma = jax.nn.sigmoid(values)
    return sigma * (1.0 + values * (1.0 - sigma))


def pad_pairs(values, row_margin):
    return jnp.pad(values, ((0, 0), (row_margin, row_margin), (2 * MAXDIL, 2 * MAXDIL)))


def tap_view(padded, row_count, rate, row_tap, col_tap, orient):
    zero_start = jnp.zeros((), jnp.int32)
    row_first = (MAXDIL + orient * row_tap * rate).astype(jnp.int32)
    col_first = (2 * MAXDIL + orient * (col_tap - row_tap) * rate).astype(jnp.int32)
    return lax.dynamic_slice(padded, (zero_start, row_first, col_first), (padded.shape[0], row_count, padded.shape[2] - 4 * MAXDIL))


def pair_inputs(extended, first, amount, band_cols):
    offsets = first + jnp.arange(amount, dtype=jnp.int32)[:, None] + jnp.arange(band_cols, dtype=jnp.int32)[None, :]
    partners = extended[offsets]
    own_rows = lax.dynamic_slice_in_dim(extended, first, amount, 0)
    product = (own_rows[:, None, :].astype(jnp.float32) * partners.astype(jnp.float32)).astype(jnp.bfloat16)
    return product, partners, own_rows, offsets


def reference(embeddings, bin_mask, target, proj_weight, dist_bias, pair_kernel, head_kernel, dilations):
    rate_pair = dilations[0]
    rate_head = dilations[1]
    extended = jnp.concatenate([embeddings, jnp.zeros((BAND, EMB), jnp.bfloat16)], 0)
    mask_ext = jnp.concatenate([bin_mask, jnp.zeros((BAND,), jnp.int32)], 0)
    partner_index = jnp.arange(BINS, dtype=jnp.int32)[:, None] + jnp.arange(BAND, dtype=jnp.int32)[None, :]
    inside = (partner_index < BINS).astype(jnp.float32)
    loss_mask = bin_mask[:, None].astype(jnp.float32) * mask_ext[partner_index].astype(jnp.float32)
    blocks = BINS // row_block

    def forward_block(index, carried):
        hidden, deriv = carried
        first = (index * row_block).astype(jnp.int32)
        product, partners, own_rows, offsets = pair_inputs(extended, first, row_block, BAND)
        pre = jnp.einsum('tde,ec->ctd', product.astype(jnp.float32), proj_weight.astype(jnp.float32))
        pre = pre + dist_bias.astype(jnp.float32)[:, None, :]
        near = lax.dynamic_slice_in_dim(inside, first, row_block, 0)
        value = (jax.nn.silu(pre) * near[None]).astype(jnp.bfloat16)
        slope_value = silu_slope(pre) * near[None]
        hidden = lax.dynamic_update_slice_in_dim(hidden, value, first, 1)
        deriv = lax.dynamic_update_slice_in_dim(deriv, slope_value, first, 1)
        return hidden, deriv

    start_forward = (jnp.zeros((CH, BINS, BAND), jnp.bfloat16), jnp.zeros((CH, BINS, BAND), jnp.float32))
    hidden_zero, deriv_zero = lax.fori_loop(0, blocks, forward_block, start_forward)
    padded_zero = pad_pairs(hidden_zero, MAXDIL)
    pre_pair = jnp.zeros((CH, BINS, BAND), jnp.float32)
    for tap, (row_tap, col_tap) in enumerate(tap_pairs):
        view = tap_view(padded_zero, BINS, rate_pair, row_tap, col_tap, 1)
        pre_pair = pre_pair + jnp.einsum('oc,cid->oid', pair_kernel[tap].astype(jnp.float32), view.astype(jnp.float32))
    hidden_one = (jax.nn.silu(pre_pair) * inside[None]).astype(jnp.bfloat16)
    deriv_one = silu_slope(pre_pair) * inside[None]
    padded_one = pad_pairs(hidden_one, MAXDIL)
    prediction = jnp.zeros((BINS, BAND), jnp.float32)
    for tap, (row_tap, col_tap) in enumerate(tap_pairs):
        view = tap_view(padded_one, BINS, rate_head, row_tap, col_tap, 1)
        prediction = prediction + jnp.einsum('c,cid->id', head_kernel[tap].astype(jnp.float32), view.astype(jnp.float32))
    residual_grad = loss_mask * (prediction - target) / BAND
    padded_grad = pad_pairs(residual_grad[None], MAXDIL)
    head_terms = []
    hidden_grad = jnp.zeros((CH, BINS, BAND), jnp.float32)
    for tap, (row_tap, col_tap) in enumerate(tap_pairs):
        view = tap_view(padded_one, BINS, rate_head, row_tap, col_tap, 1)
        head_terms.append(jnp.einsum('cid,id->c', view.astype(jnp.float32), residual_grad))
        back_view = tap_view(padded_grad, BINS, rate_head, row_tap, col_tap, -1)
        hidden_grad = hidden_grad + head_kernel[tap].astype(jnp.float32)[:, None, None] * back_view
    head_grad = jnp.stack(head_terms) / BINS
    slope_one = (hidden_grad * deriv_one).astype(jnp.bfloat16)
    padded_slope = pad_pairs(slope_one, MAXDIL)
    pair_terms = []
    zero_grad = jnp.zeros((CH, BINS, BAND), jnp.float32)
    for tap, (row_tap, col_tap) in enumerate(tap_pairs):
        view = tap_view(padded_zero, BINS, rate_pair, row_tap, col_tap, 1)
        pair_terms.append(jnp.einsum('oid,cid->oc', slope_one.astype(jnp.float32), view.astype(jnp.float32)))
        back_view = tap_view(padded_slope, BINS, rate_pair, row_tap, col_tap, -1)
        zero_grad = zero_grad + jnp.einsum('oc,oid->cid', pair_kernel[tap].astype(jnp.float32), back_view.astype(jnp.float32))
    pair_grad = jnp.stack(pair_terms) / BINS
    slope_zero = (zero_grad * deriv_zero).astype(jnp.bfloat16)

    def backward_block(index, carried):
        proj_acc, grad_ext = carried
        first = (index * row_block).astype(jnp.int32)
        product, partners, own_rows, offsets = pair_inputs(extended, first, row_block, BAND)
        piece_rows = lax.dynamic_slice_in_dim(slope_zero, first, row_block, 1)
        proj_acc = proj_acc + jnp.einsum('tde,ctd->ec', product.astype(jnp.float32), piece_rows.astype(jnp.float32))
        slope = jnp.einsum('ctd,ec->tde', piece_rows.astype(jnp.float32), proj_weight.astype(jnp.float32))
        own_term = jnp.sum(slope * partners.astype(jnp.float32), axis=1)
        grad_ext = grad_ext.at[offsets].add(slope * own_rows.astype(jnp.float32)[:, None, :])
        current = lax.dynamic_slice_in_dim(grad_ext, first, row_block, 0)
        grad_ext = lax.dynamic_update_slice_in_dim(grad_ext, current + own_term, first, 0)
        return proj_acc, grad_ext

    start_state = (jnp.zeros((EMB, CH), jnp.float32), jnp.zeros((BINS + BAND, EMB), jnp.float32))
    proj_acc, grad_ext = lax.fori_loop(0, blocks, backward_block, start_state)
    return grad_ext[:BINS], proj_acc / BINS, pair_grad, head_grad
```

```python
import functools

import jax
import jax.numpy as jnp
from jax import lax
from jax.experimental import pallas as pl
from jax.experimental.pallas import tpu as pltpu
from jax.sharding import Mesh, PartitionSpec as P

F32 = jnp.float32
BF16 = jnp.bfloat16
EMB = 512
CH = 64
BAND = 256
BINS = 4096
OWN = 16
HALO = 16
ROWS = OWN + 2 * HALO
WIDE = 384
GENOME = ("yl", "x", "z", "core")
CHIPS = ("yl", "x", "z")
NT = (((1,), (1,)), ((), ()))
TN = (((0,), (0,)), ((), ()))


def dot(a, b, dims=(((1,), (0,)), ((), ()))):
    return lax.dot_general(a, b, dims, preferred_element_type=F32)


def sigmoid(v):
    return 0.5 * jnp.tanh(0.5 * v) + 0.5


def kernel(
    scalars, win, wt, bias, kf, kb, hk, hkt, tgt,
    g_out, w_out,
    et, ef, mrow, cmask, pre, hz, d0, h1, d1, s1, s1b, sz, aown, q, rgb, tgw, pacc, g1, pg, hg,
):
    r0 = scalars[0]
    r1 = scalars[1]
    w0 = scalars[2]
    col = lax.broadcasted_iota(jnp.int32, (1, WIDE), 1)

    def band(r):
        high = jnp.where(w0 + r >= 0, jnp.minimum(r + BAND, BINS - w0), 0)
        return jnp.where((col >= r) & (col < high), 1.0, 0.0).astype(F32)

    def back_roll(v, by):
        return pltpu.roll(v, WIDE - by, 1)

    wide = win[:, :EMB].astype(F32)
    et[...] = wide.T.astype(BF16)
    ef[...] = wide[:ROWS]
    marks = win[:, EMB:].astype(F32)
    mrow[...] = marks[:ROWS]
    cmask[...] = marks.T[:8]
    padded = jnp.concatenate([tgt[...], jnp.zeros((32, WIDE - BAND), F32)], 1)
    tgw[...] = pltpu.roll(padded, 8, 1, stride=1, stride_axis=0)

    def forward(b, _):
        e8 = ef[pl.ds(pl.multiple_of(b * 8, 8), 8), :]
        w = wt[...].astype(F32)
        a = jnp.concatenate([(w * e8[k : k + 1]).astype(BF16) for k in range(8)], 0)

        @pl.when((b >= 2) & (b < 4))
        def _():
            aown[pl.ds(pl.multiple_of((b - 2) * 512, 512), 512), :] = a

        pre[...] = dot(a, et[...])

        def row(k, _):
            r = b * 8 + k
            v = pre[pl.ds(pl.multiple_of(k * CH, CH), CH), :] + pltpu.roll(bias[...], r, 1)
            s = sigmoid(v)
            m = band(r)
            hz[r] = (v * s * m).astype(BF16)

            @pl.when((r >= HALO) & (r < HALO + OWN))
            def _():
                d0[r - HALO] = s * (1.0 + v * (1.0 - s)) * m

            return 0

        lax.fori_loop(0, 8, row, 0)
        return 0

    lax.fori_loop(0, ROWS // 8, forward, 0)

    def second(n, _):
        for k in range(4):
            r = 4 + n * 4 + k
            near = jnp.concatenate([hz[r - r0], hz[r], hz[r + r0]], 0)
            p = dot(kf[...], near)
            v = pltpu.roll(p[:CH], r0, 1) + p[CH : 2 * CH] + back_roll(p[2 * CH :], r0)
            s = sigmoid(v)
            m = band(r)
            one = (v * s * m).astype(BF16)
            h1[r] = one
            d1[r] = s * (1.0 + v * (1.0 - s)) * m
            p9 = dot(hk[...], one)
            q[r] = pltpu.roll(p9[:8], r1, 1) + p9[8:16] + back_roll(p9[16:24], r1)
        return 0

    lax.fori_loop(0, 10, second, 0)

    which = lax.broadcasted_iota(jnp.int32, (8, WIDE), 0)

    def residual(n, _):
        for k in range(4):
            r = 8 + n * 4 + k
            pred = q[r - r1][0:1] + q[r][1:2] + q[r + r1][2:3]
            mark = mrow[pl.ds(r, 1), :]
            lm = jnp.concatenate([mark] * (WIDE // 128), 1) * cmask[0:1] * band(r)
            rg = lm * (pred - tgw[pl.ds(r - 8, 1), :]) * (1.0 / BAND)
            rg = jnp.broadcast_to(rg, (8, WIDE))
            taps = jnp.where(
                which == 0,
                back_roll(rg, r1),
                jnp.where(which == 1, rg, jnp.where(which == 2, pltpu.roll(rg, r1, 1), 0.0)),
            )
            high = taps.astype(BF16).astype(F32)
            rgb[r] = jnp.concatenate([high, taps - high], 0).astype(BF16)
        return 0

    lax.fori_loop(0, 8, residual, 0)

    def slope(n, _):
        for k in range(4):
            r = 12 + n * 4 + k
            near = jnp.concatenate([rgb[r + r1], rgb[r], rgb[r - r1]], 0)
            s = (dot(hkt[...], near) * d1[r]).astype(BF16)
            s1[r] = s

            @pl.when((r >= HALO) & (r < HALO + OWN))
            def _():
                sf = s.astype(F32)
                s1b[r - HALO] = jnp.concatenate(
                    [back_roll(sf, r0).astype(BF16), s, pltpu.roll(sf, r0, 1).astype(BF16)], 0
                )

        return 0

    lax.fori_loop(0, 6, slope, 0)

    pg[...] = jnp.zeros_like(pg)
    hg[...] = jnp.zeros_like(hg)

    def grads(n, _):
        psum, hsum = 0.0, 0.0
        for k in range(4):
            i = n * 4 + k
            r = HALO + i
            near = jnp.concatenate([hz[r - r0], hz[r], hz[r + r0]], 0)
            psum = psum + dot(s1b[i], near, NT)
            near = jnp.concatenate([h1[r - r1], h1[r], h1[r + r1]], 0)
            hsum = hsum + dot(rgb[r], near, NT)
            near = jnp.concatenate([s1[r + r0], s1[r], s1[r - r0]], 0)
            p = dot(kb[...], near)
            zg = back_roll(p[:CH], r0) + p[CH : 2 * CH] + pltpu.roll(p[2 * CH :], r0, 1)
            sz[pl.ds(pl.multiple_of(i * CH, CH), CH), :] = (zg * d0[i]).astype(BF16)
        pg[...] += psum
        hg[...] += hsum
        return 0

    lax.fori_loop(0, 4, grads, 0)

    pacc[...] = jnp.zeros_like(pacc)

    def back(n, _):
        t = dot(sz[pl.ds(pl.multiple_of(n * 256, 256), 256), :], win[:, :EMB])
        w = wt[...].astype(F32)
        acc = pacc[...]
        for k in range(4):
            tr = t[k * CH : (k + 1) * CH]
            g1[pl.ds(n * 4 + k, 1), :] = jnp.sum(w * tr, axis=0, keepdims=True)
            acc = acc + tr * ef[pl.ds(HALO + n * 4 + k, 1), :]
        pacc[...] = acc
        return 0

    lax.fori_loop(0, 4, back, 0)
    g = dot(sz[...], aown[...], TN)
    g_out[...] = g.astype(BF16)
    g_out[HALO : HALO + OWN, :] = (g[HALO : HALO + OWN] + g1[...]).astype(BF16)

    w_out[...] = jnp.zeros_like(w_out)
    heads = hg[0:8] + hg[8:16]
    for half in range(2):
        t = 0
        for a in range(4):
            for b in range(4):
                w_out[half, t] = pacc[half * 32 + a * 8 : half * 32 + a * 8 + 8, b * 128 : b * 128 + 128]
                t += 1
        for b in range(3):
            for a in range(4):
                rows = pg[b * CH + half * 32 + a * 8 : b * CH + half * 32 + a * 8 + 8, :]
                w_out[half, t] = rows[:, :128]
                w_out[half, t + 1, :, : 3 * CH - 128] = rows[:, 128:]
                t += 2
        w_out[half, t] = heads[:, :128]
        w_out[half, t + 1, :, : 3 * CH - 128] = heads[:, 128:]


def run_kernel(scalars, win, wt, bias, kf, kb, hk, hkt, tgt):
    vmem = pl.BlockSpec(memory_space=pltpu.VMEM)
    return pl.pallas_call(
        kernel,
        out_shape=(
            jax.ShapeDtypeStruct((WIDE, EMB), BF16),
            jax.ShapeDtypeStruct((2, 64, 8, 128), F32),
        ),
        in_specs=[pl.BlockSpec(memory_space=pltpu.SMEM)] + [vmem] * 8,
        out_specs=(vmem, vmem),
        scratch_shapes=[
            pltpu.VMEM((EMB, WIDE), BF16),
            pltpu.VMEM((ROWS, EMB), F32),
            pltpu.VMEM((ROWS, 128), F32),
            pltpu.VMEM((8, WIDE), F32),
            pltpu.VMEM((8 * CH, WIDE), F32),
            pltpu.VMEM((ROWS, CH, WIDE), BF16),
            pltpu.VMEM((OWN, CH, WIDE), F32),
            pltpu.VMEM((ROWS, CH, WIDE), BF16),
            pltpu.VMEM((ROWS, CH, WIDE), F32),
            pltpu.VMEM((ROWS, CH, WIDE), BF16),
            pltpu.VMEM((OWN, 3 * CH, WIDE), BF16),
            pltpu.VMEM((OWN * CH, WIDE), BF16),
            pltpu.VMEM((OWN * CH, EMB), BF16),
            pltpu.VMEM((ROWS, 8, WIDE), F32),
            pltpu.VMEM((ROWS, 16, WIDE), BF16),
            pltpu.VMEM((32, WIDE), F32),
            pltpu.VMEM((CH, EMB), F32),
            pltpu.VMEM((OWN, EMB), F32),
            pltpu.VMEM((3 * CH, 3 * CH), F32),
            pltpu.VMEM((16, 3 * CH), F32),
        ],
        compiler_params=pltpu.CompilerParams(vmem_limit_bytes=48 * 1024 * 1024),
    )(scalars, win, wt, bias, kf, kb, hk, hkt, tgt)


def both(value, chan):
    other = lax.ppermute(value, "chan", [(0, 1), (1, 0)])
    return jnp.where(chan == 0, jnp.stack([value, other]), jnp.stack([other, value]))


def swap(value, axis):
    return lax.ppermute(value, axis, [(0, 1), (1, 0)])


def local(sizes, embeddings, bin_mask, target, proj_weight, dist_bias, pair_kernel, head_kernel, dilations):
    chips = sizes["yl"] * sizes["x"] * sizes["z"]
    chan = lax.axis_index("chan")
    core = lax.axis_index("core")
    first = (lax.axis_index(GENOME) * 2 + chan) * OWN

    packed = jnp.concatenate(
        [
            proj_weight.T.reshape(-1, 128),
            dist_bias.reshape(-1, 128),
            pair_kernel.transpose(1, 0, 2).reshape(-1, 128),
            jnp.pad(head_kernel.T.reshape(-1), (0, 96)).reshape(-1, 128),
        ],
        0,
    )
    pair = both(packed, chan)
    at = 0

    def take(rows, shape):
        nonlocal at
        piece = pair[:, at : at + rows]
        at += rows
        return piece.reshape((2,) + shape)

    wt = take(128, (32, EMB)).reshape(CH, EMB)
    bias = take(64, (32, BAND)).reshape(CH, BAND)
    kernels = take(144, (32, 3, 3, CH)).reshape(CH, 3, 3, CH)
    heads = pair[:, at : at + 3].reshape(2, 384)[:, :288].reshape(CH, 3, 3)
    bias = jnp.pad(bias.astype(F32), ((0, 0), (0, WIDE - BAND)))
    kf = kernels.transpose(2, 0, 1, 3).reshape(3 * CH, 3 * CH)
    kb = kernels.transpose(2, 3, 1, 0).reshape(3 * CH, 3 * CH)
    hk = jnp.pad(heads.transpose(2, 1, 0), ((0, 0), (0, 5), (0, 0))).reshape(24, CH)
    hkt = jnp.pad(heads, ((0, 0), (0, 0), (0, 5)))
    hkt = jnp.concatenate([hkt, hkt], 2).reshape(CH, 48)

    marked = jnp.concatenate(
        [embeddings, jnp.broadcast_to(bin_mask.astype(BF16)[:, None], (2 * OWN, 128))], 1
    )

    def ahead(value, by):
        return lax.ppermute(value, CHIPS, [(i, i - by) for i in range(by, chips)])

    same = [marked] + [ahead(marked, n) for n in range(1, 5)]
    flat = lambda chip, c, h: (chip * 2 + c) * 2 + h
    rim_pairs = [(flat(i, 1, 0), flat(i + 1, 0, 0)) for i in range(chips - 1)]
    rim_pairs += [(flat(i, 0, 1), flat(i - 5, 1, 1)) for i in range(5, chips)]
    rim = lax.ppermute(
        jnp.where(core == 0, marked[:OWN], marked[OWN:]), GENOME + ("chan",), rim_pairs
    )
    sibling = [swap(value, "core") for value in same]
    zero_half = jnp.zeros((OWN, marked.shape[1]), BF16)
    window_even = []
    for a, b in zip(same, sibling):
        window_even += [a, b]
    window_odd = [same[0]]
    for n in range(1, 5):
        window_odd += [sibling[n], same[n]]
    even = jnp.concatenate(window_even[:9], 0)
    odd = jnp.concatenate(window_odd, 0)
    main = jnp.where(core == 0, even, odd)
    before = jnp.where(core == 0, rim, sibling[0][OWN:])
    after = jnp.where(core == 0, sibling[4][:OWN], rim)
    fill = jnp.zeros((WIDE - 304, marked.shape[1]), BF16)
    win = jnp.where(
        chan == 0,
        jnp.concatenate([before, main, fill], 0),
        jnp.concatenate([main, after, fill], 0),
    )

    genome = chips * 2
    target_pairs = [(2 * i, 2 * i + 2) for i in range(genome - 1)]
    target_pairs += [(2 * i + 1, 2 * i - 1) for i in range(1, genome)]
    rim_target = lax.ppermute(
        jnp.where(chan == 0, target[24:], target[:8]), GENOME + ("chan",), target_pairs
    )
    tgt = jnp.where(
        chan == 0,
        jnp.concatenate([rim_target, target[:24]], 0),
        jnp.concatenate([target[8:], rim_target], 0),
    )

    scalars = jnp.stack([dilations[0], dilations[1], first - HALO]).astype(jnp.int32)
    g, w = run_kernel(scalars, win, wt, bias, kf, kb, hk, hkt, tgt)

    lead = jnp.zeros((OWN, EMB), BF16)
    blocks = jnp.where(
        chan == 0, g[HALO : HALO + 288], jnp.concatenate([lead, g[HALO : HALO + 272]], 0)
    ).reshape(9, 2 * OWN, EMB)
    kept = blocks[0::2].astype(F32)
    given = swap(blocks[1::2], "core").astype(F32)
    none = jnp.zeros((1, 2 * OWN, EMB), F32)
    kept = kept + jnp.where(
        core == 0, jnp.concatenate([none, given], 0), jnp.concatenate([given, none], 0)
    )
    mine = jnp.where(chan == 0, kept[..., :256], kept[..., 256:])
    others = jnp.where(chan == 0, kept[..., 256:], kept[..., :256]).astype(BF16)
    mine = mine + swap(others, "chan").astype(F32)
    total = mine[0]
    for n in range(1, 5):
        moved = lax.ppermute(
            mine[n].astype(BF16), CHIPS, [(i, i + n) for i in range(chips - n)]
        )
        total = total + moved.astype(F32)

    mine_w = jnp.where(chan == 0, w[0], w[1])
    other_w = jnp.where(chan == 0, w[1], w[0])
    mine_w = mine_w + swap(other_w, "chan")
    tiles = 64
    mine_w = mine_w + swap(mine_w, "core")
    pieces = lax.all_to_all(mine_w.reshape(chips, tiles // chips * 8, 128), CHIPS, 0, 0, tiled=True)
    piece = jnp.sum(pieces, axis=0, keepdims=True)
    whole = lax.all_to_all(
        jnp.broadcast_to(piece, (chips,) + piece.shape[1:]), CHIPS, 0, 0, tiled=True
    ).reshape(tiles, 8, 128)
    whole = whole * (1.0 / BINS)
    proj = whole[:16].reshape(4, 4, 8, 128).transpose(1, 3, 0, 2).reshape(EMB, 32)
    conv = whole[16:40].reshape(3, 4, 2, 8, 128).transpose(0, 1, 3, 2, 4).reshape(3, 32, 256)
    conv = conv[:, :, : 3 * CH].reshape(3, 32, 3, CH)
    conv = conv.transpose(2, 0, 1, 3).reshape(9, 32, CH)
    head = whole[40:42].transpose(1, 0, 2).reshape(8, 256)[:3, : 3 * CH].reshape(3, 3, CH)
    head = head.transpose(1, 0, 2).reshape(9, CH)
    head = jnp.where(chan == 0, head[:, :32], head[:, 32:])
    return total, proj, conv, head


def solution(mesh):
    split = mesh.devices.reshape(2, 4, 8, 2, 2)
    sizes = dict(yl=2, x=4, z=8, core=2, chan=2)
    fine = Mesh(split, ("yl", "x", "z", "core", "chan"))
    return jax.shard_map(
        functools.partial(local, sizes),
        mesh=fine,
        in_specs=(
            P(GENOME, None),
            P(GENOME),
            P(GENOME, None),
            P(None, "chan"),
            P("chan", None),
            P(None, "chan", None),
            P(None, "chan"),
            P(),
        ),
        out_specs=(P(GENOME, "chan"), P(None, "chan"), P(None, "chan", None), P(None, "chan")),
        check_vma=False,
    )
```

```python
import functools

import jax
import jax.numpy as jnp
from jax import lax
from jax.experimental import pallas as pl
from jax.experimental.pallas import tpu as pltpu
from jax.sharding import Mesh, PartitionSpec as P

F32 = jnp.float32
BF16 = jnp.bfloat16
EMB = 512
CH = 64
HALF = CH // 2
BAND = 256
BINS = 4096
BLOCK = 32
OWN = 16
HALO = 16
ROWS = OWN + 2 * HALO
WIDE = 384
LEAD = 32
PACK = 96
MARKED = EMB + 128
PIECE = 384
AHEAD = 5
GENOME = ("yl", "x", "z", "core")
CHIPS = ("yl", "x", "z")
ALL = GENOME + ("chan",)
NT = (((1,), (1,)), ((), ()))
TN = (((0,), (0,)), ((), ()))


def dot(a, b, dims=(((1,), (0,)), ((), ()))):
    return lax.dot_general(a, b, dims, preferred_element_type=F32)


def sigmoid(v):
    return 0.5 * jnp.tanh(0.5 * v) + 0.5


def pack_kernel(emb, mask, proj, bias, pair, head, marked, packed):
    marked[:, :EMB] = emb[...]
    line = jnp.broadcast_to(mask[...].astype(F32), (BLOCK, BLOCK))
    row = lax.broadcasted_iota(jnp.int32, (BLOCK, BLOCK), 0)
    own = jnp.where(row == lax.broadcasted_iota(jnp.int32, (BLOCK, BLOCK), 1), line, 0.0)
    column = jnp.sum(own, axis=1, keepdims=True)
    marked[:, EMB:] = jnp.broadcast_to(column, (BLOCK, 128)).astype(BF16)
    packed[:HALF, :] = proj[...]
    packed[32:48, :] = jnp.concatenate([bias[:16], bias[16:]], 1)
    taps = [pair[tap].astype(F32) for tap in range(9)]
    packed[48:80, :] = jnp.concatenate(taps[:8], 1).astype(BF16)
    last = jnp.concatenate([taps[8][:16], taps[8][16:]], 1)
    heads = jnp.concatenate([head[...].astype(F32), jnp.zeros((7, HALF), F32)], 0)
    rest = jnp.zeros((16, EMB - 128 - HALF), F32)
    packed[80:96, :] = jnp.concatenate([last, heads, rest], 1).astype(BF16)


def kernel(scalars, *refs):
    same, sibling = refs[:AHEAD], refs[AHEAD : 2 * AHEAD]
    (
        rim, own_pack, other_pack, target, rim_target,
        keep_out, give_out, w_out,
        window, wt, bias, kf, kb, hk, hkt,
        et, ef, mrow, cmask, pre, hz, d0, h1, d1, s1, s1b, sz, aown, q, rgb, tgw, pacc, g1, pg, hg, gs,
    ) = refs[2 * AHEAD :]
    r0 = scalars[0]
    r1 = scalars[1]
    w0 = scalars[2]
    core = scalars[3]
    chan = scalars[4]
    col = lax.broadcasted_iota(jnp.int32, (1, WIDE), 1)

    def band(r):
        high = jnp.where(w0 + r >= 0, jnp.minimum(r + BAND, BINS - w0), 0)
        return jnp.where((col >= r) & (col < high), 1.0, 0.0).astype(F32)

    def back_roll(v, by):
        return pltpu.roll(v, WIDE - by, 1)

    window[...] = jnp.zeros_like(window)
    for n in range(AHEAD):
        at = LEAD + 64 * n + HALO - OWN * chan
        window[pl.ds(pl.multiple_of(at, 16), BLOCK), :] = same[n][...]
        at = at + BLOCK * (1 - 2 * core)
        window[pl.ds(pl.multiple_of(at, 16), BLOCK), :] = sibling[n][...]

    @pl.when((core == 0) & (chan == 0))
    def _():
        window[LEAD : LEAD + OWN, :] = rim[...]

    @pl.when((core == 1) & (chan == 1))
    def _():
        window[LEAD + 288 : LEAD + 304, :] = rim[...]

    win = window.at[LEAD : LEAD + WIDE]

    flip = jnp.full((PACK, EMB), chan, jnp.int32) == 0
    mine, other = own_pack[...].astype(F32), other_pack[...].astype(F32)
    halves = [jnp.where(flip, mine, other), jnp.where(flip, other, mine)]
    wt[...] = jnp.concatenate([h[:HALF] for h in halves], 0)
    rows = []
    for h in halves:
        rows += [h[32:48, :BAND], h[32:48, BAND:]]
    bias[...] = jnp.concatenate(
        [jnp.concatenate(rows, 0), jnp.zeros((CH, WIDE - BAND), F32)], 1
    )
    taps = []
    for tap in range(9):
        parts = []
        for h in halves:
            if tap < 8:
                parts.append(h[48:80, tap * CH : tap * CH + CH])
            else:
                parts += [h[80:96, :CH], h[80:96, CH : 2 * CH]]
        taps.append(jnp.concatenate(parts, 0))
    grid = lambda pick: jnp.concatenate(
        [jnp.concatenate([taps[pick(n, m)] for m in range(3)], 1) for n in range(3)], 0
    )
    kf[...] = grid(lambda b, a: 3 * a + b).astype(BF16)
    kb[...] = grid(lambda a, b: 3 * a + b).T.astype(BF16)
    heads = jnp.concatenate([h[80:96, 128 : 128 + HALF] for h in halves], 1)
    rest = jnp.zeros((5, CH), F32)
    rows = []
    for b in range(3):
        rows += [heads[3 * a + b : 3 * a + b + 1] for a in range(3)] + [rest]
    hk[...] = jnp.concatenate(rows, 0).astype(BF16)
    rows = []
    for a in range(3):
        rows += [heads[3 * a : 3 * a + 3], rest] * 2
    hkt[...] = jnp.concatenate(rows, 0).T.astype(BF16)

    wide = win[:, :EMB].astype(F32)
    et[...] = wide.T.astype(BF16)
    ef[...] = wide[:ROWS]
    marks = win[:, EMB:].astype(F32)
    mrow[...] = marks[:ROWS]
    cmask[...] = marks.T[:8]

    tgt = jnp.where(
        jnp.full((BLOCK, BAND), chan, jnp.int32) == 0,
        jnp.concatenate([rim_target[...], target[:24]], 0),
        jnp.concatenate([target[8:], rim_target[...]], 0),
    )
    padded = jnp.concatenate([tgt, jnp.zeros((BLOCK, WIDE - BAND), F32)], 1)
    tgw[...] = pltpu.roll(padded, 8, 1, stride=1, stride_axis=0)

    def forward(b, _):
        e8 = ef[pl.ds(pl.multiple_of(b * 8, 8), 8), :]
        w = wt[...]
        a = jnp.concatenate([(w * e8[k : k + 1]).astype(BF16) for k in range(8)], 0)

        @pl.when((b >= 2) & (b < 4))
        def _():
            aown[pl.ds(pl.multiple_of((b - 2) * 512, 512), 512), :] = a

        pre[...] = dot(a, et[...])

        def row(k, _):
            r = b * 8 + k
            v = pre[pl.ds(pl.multiple_of(k * CH, CH), CH), :] + pltpu.roll(bias[...], r, 1)
            s = sigmoid(v)
            m = band(r)
            hz[r] = (v * s * m).astype(BF16)

            @pl.when((r >= HALO) & (r < HALO + OWN))
            def _():
                d0[r - HALO] = s * (1.0 + v * (1.0 - s)) * m

            return 0

        lax.fori_loop(0, 8, row, 0)
        return 0

    lax.fori_loop(0, ROWS // 8, forward, 0)

    def second(n, _):
        for k in range(4):
            r = 4 + n * 4 + k
            near = jnp.concatenate([hz[r - r0], hz[r], hz[r + r0]], 0)
            p = dot(kf[...], near)
            v = pltpu.roll(p[:CH], r0, 1) + p[CH : 2 * CH] + back_roll(p[2 * CH :], r0)
            s = sigmoid(v)
            m = band(r)
            one = (v * s * m).astype(BF16)
            h1[r] = one
            d1[r] = s * (1.0 + v * (1.0 - s)) * m
            p9 = dot(hk[...], one)
            q[r] = pltpu.roll(p9[:8], r1, 1) + p9[8:16] + back_roll(p9[16:24], r1)
        return 0

    lax.fori_loop(0, 10, second, 0)

    which = lax.broadcasted_iota(jnp.int32, (8, WIDE), 0)

    def residual(n, _):
        for k in range(4):
            r = 8 + n * 4 + k
            pred = q[r - r1][0:1] + q[r][1:2] + q[r + r1][2:3]
            mark = mrow[pl.ds(r, 1), :]
            lm = jnp.concatenate([mark] * (WIDE // 128), 1) * cmask[0:1] * band(r)
            rg = lm * (pred - tgw[pl.ds(r - 8, 1), :]) * (1.0 / BAND)
            rg = jnp.broadcast_to(rg, (8, WIDE))
            taps = jnp.where(
                which == 0,
                back_roll(rg, r1),
                jnp.where(which == 1, rg, jnp.where(which == 2, pltpu.roll(rg, r1, 1), 0.0)),
            )
            high = taps.astype(BF16).astype(F32)
            rgb[r] = jnp.concatenate([high, taps - high], 0).astype(BF16)
        return 0

    lax.fori_loop(0, 8, residual, 0)

    def slope(n, _):
        for k in range(4):
            r = 12 + n * 4 + k
            near = jnp.concatenate([rgb[r + r1], rgb[r], rgb[r - r1]], 0)
            s = (dot(hkt[...], near) * d1[r]).astype(BF16)
            s1[r] = s

            @pl.when((r >= HALO) & (r < HALO + OWN))
            def _():
                sf = s.astype(F32)
                s1b[r - HALO] = jnp.concatenate(
                    [back_roll(sf, r0).astype(BF16), s, pltpu.roll(sf, r0, 1).astype(BF16)], 0
                )

        return 0

    lax.fori_loop(0, 6, slope, 0)

    pg[...] = jnp.zeros_like(pg)
    hg[...] = jnp.zeros_like(hg)

    def grads(n, _):
        psum, hsum = 0.0, 0.0
        for k in range(4):
            i = n * 4 + k
            r = HALO + i
            near = jnp.concatenate([hz[r - r0], hz[r], hz[r + r0]], 0)
            psum = psum + dot(s1b[i], near, NT)
            near = jnp.concatenate([h1[r - r1], h1[r], h1[r + r1]], 0)
            hsum = hsum + dot(rgb[r], near, NT)
            near = jnp.concatenate([s1[r + r0], s1[r], s1[r - r0]], 0)
            p = dot(kb[...], near)
            zg = back_roll(p[:CH], r0) + p[CH : 2 * CH] + pltpu.roll(p[2 * CH :], r0, 1)
            sz[pl.ds(pl.multiple_of(i * CH, CH), CH), :] = (zg * d0[i]).astype(BF16)
        pg[...] += psum
        hg[...] += hsum
        return 0

    lax.fori_loop(0, 4, grads, 0)

    pacc[...] = jnp.zeros_like(pacc)

    def back(n, _):
        t = dot(sz[pl.ds(pl.multiple_of(n * 256, 256), 256), :], win[:, :EMB])
        w = wt[...]
        acc = pacc[...]
        for k in range(4):
            tr = t[k * CH : (k + 1) * CH]
            g1[pl.ds(n * 4 + k, 1), :] = jnp.sum(w * tr, axis=0, keepdims=True)
            acc = acc + tr * ef[pl.ds(HALO + n * 4 + k, 1), :]
        pacc[...] = acc
        return 0

    lax.fori_loop(0, 4, back, 0)
    g = dot(sz[...], aown[...], TN)
    gs[...] = g
    gs[HALO : HALO + OWN, :] = g[HALO : HALO + OWN] + g1[...]
    for n in range(2 * AHEAD - 1):
        block = gs[pl.ds(pl.multiple_of(BLOCK * n + HALO - OWN * chan, 16), BLOCK), :]
        if n % 2:
            give_out[n // 2] = block.astype(BF16)
        else:
            keep_out[n // 2] = block

    heads = hg[0:8] + hg[8:16]
    blank = jnp.zeros((8, 256 - 3 * CH), F32)
    for half in range(2):
        tiles = []
        for a in range(4):
            for b in range(4):
                tiles.append(pacc[half * 32 + a * 8 : half * 32 + a * 8 + 8, b * 128 : b * 128 + 128])
        for b in range(3):
            for a in range(4):
                at = b * CH + half * 32 + a * 8
                row = jnp.concatenate([pg[at : at + 8, :], blank], 1)
                tiles += [row[:, :128], row[:, 128:]]
        row = jnp.concatenate([heads, blank], 1)
        tiles += [row[:, :128], row[:, 128:]]
        tiles += [jnp.zeros((8, 128), F32)] * (48 - len(tiles))
        for t, tile in enumerate(tiles):
            at, lane = half * 64 + t % 24 // 3 * 8, t % 3 * 128
            w_out[t // 24, at : at + 8, lane : lane + 128] = tile


VMEM = pl.BlockSpec(memory_space=pltpu.VMEM)
SMEM = pl.BlockSpec(memory_space=pltpu.SMEM)


def run_pack(*args):
    return pl.pallas_call(
        pack_kernel,
        out_shape=(
            jax.ShapeDtypeStruct((BLOCK, MARKED), BF16),
            jax.ShapeDtypeStruct((PACK, EMB), BF16),
        ),
        in_specs=[VMEM] * len(args),
        out_specs=(VMEM, VMEM),
    )(*args)


def run_kernel(*args):
    return pl.pallas_call(
        kernel,
        out_shape=(
            jax.ShapeDtypeStruct((AHEAD, BLOCK, EMB), F32),
            jax.ShapeDtypeStruct((AHEAD - 1, BLOCK, EMB), BF16),
            jax.ShapeDtypeStruct((2, 128, PIECE), F32),
        ),
        in_specs=[SMEM] + [VMEM] * (len(args) - 1),
        out_specs=(VMEM, VMEM, VMEM),
        scratch_shapes=[
            pltpu.VMEM((LEAD + WIDE, MARKED), BF16),
            pltpu.VMEM((CH, EMB), F32),
            pltpu.VMEM((CH, WIDE), F32),
            pltpu.VMEM((3 * CH, 3 * CH), BF16),
            pltpu.VMEM((3 * CH, 3 * CH), BF16),
            pltpu.VMEM((24, CH), BF16),
            pltpu.VMEM((CH, 48), BF16),
            pltpu.VMEM((EMB, WIDE), BF16),
            pltpu.VMEM((ROWS, EMB), F32),
            pltpu.VMEM((ROWS, 128), F32),
            pltpu.VMEM((8, WIDE), F32),
            pltpu.VMEM((8 * CH, WIDE), F32),
            pltpu.VMEM((ROWS, CH, WIDE), BF16),
            pltpu.VMEM((OWN, CH, WIDE), F32),
            pltpu.VMEM((ROWS, CH, WIDE), BF16),
            pltpu.VMEM((ROWS, CH, WIDE), F32),
            pltpu.VMEM((ROWS, CH, WIDE), BF16),
            pltpu.VMEM((OWN, 3 * CH, WIDE), BF16),
            pltpu.VMEM((OWN * CH, WIDE), BF16),
            pltpu.VMEM((OWN * CH, EMB), BF16),
            pltpu.VMEM((ROWS, 8, WIDE), F32),
            pltpu.VMEM((ROWS, 16, WIDE), BF16),
            pltpu.VMEM((BLOCK, WIDE), F32),
            pltpu.VMEM((CH, EMB), F32),
            pltpu.VMEM((OWN, EMB), F32),
            pltpu.VMEM((3 * CH, 3 * CH), F32),
            pltpu.VMEM((16, 3 * CH), F32),
            pltpu.VMEM((WIDE, EMB), F32),
        ],
        compiler_params=pltpu.CompilerParams(vmem_limit_bytes=48 * 1024 * 1024),
    )(*args)


def final_kernel(scalars, own, other, proj_out, pair_out, head_out):
    core = scalars[3]
    chan = scalars[4]
    flip = jnp.full((64, PIECE), core, jnp.int32) == 0
    mine, theirs = own[...], other[...]
    scale = 1.0 / BINS
    both = [jnp.where(flip, mine, theirs) * scale, jnp.where(flip, theirs, mine) * scale]

    def tile(t):
        at, lane = t % 24 // 3 * 8, t % 3 * 128
        return both[t // 24][at : at + 8, lane : lane + 128]

    proj = [jnp.concatenate([tile(4 * a + b) for b in range(4)], 1) for a in range(4)]
    proj_out[...] = jnp.concatenate(proj, 0)
    for b in range(3):
        for a in range(4):
            t = 16 + (b * 4 + a) * 2
            row = jnp.concatenate([tile(t), tile(t + 1)], 1)
            for k in range(3):
                pair_out[3 * k + b, 8 * a : 8 * a + 8, :] = row[:, CH * k : CH * k + CH]
    row = jnp.concatenate([tile(40), tile(41)], 1)
    for k in range(3):
        line = row[:3, CH * k : CH * k + CH]
        first = jnp.full((3, HALF), chan, jnp.int32) == 0
        head_out[3 * k : 3 * k + 3, :] = jnp.where(first, line[:, :HALF], line[:, HALF:])


def run_final(*args):
    return pl.pallas_call(
        final_kernel,
        out_shape=(
            jax.ShapeDtypeStruct((HALF, EMB), F32),
            jax.ShapeDtypeStruct((9, HALF, CH), F32),
            jax.ShapeDtypeStruct((9, HALF), F32),
        ),
        in_specs=[SMEM] + [VMEM] * (len(args) - 1),
        out_specs=(VMEM, VMEM, VMEM),
    )(*args)


def swap(value, axis):
    return lax.ppermute(value, axis, [(0, 1), (1, 0)])


def cycle(value, axes, length, by):
    return lax.ppermute(value, axes, [(i, (i + by) % length) for i in range(length)])


def exchange(value, axes):
    return lax.all_to_all(value, axes, 0, 0, tiled=True)


def local(sizes, embeddings, bin_mask, target, proj_weight, dist_bias, pair_kernel, head_kernel, dilations):
    chips = sizes["yl"] * sizes["x"] * sizes["z"]
    chan = lax.axis_index("chan")
    core = lax.axis_index("core")
    first = (lax.axis_index(GENOME) * 2 + chan) * OWN
    scalars = jnp.stack([dilations[0], dilations[1], first - HALO, core, chan]).astype(jnp.int32)

    marked, packed = run_pack(
        embeddings, bin_mask[None, :], proj_weight.T, dist_bias, pair_kernel, head_kernel
    )
    other_pack = swap(packed, "chan")
    same = [marked] + [cycle(marked, CHIPS, chips, -n) for n in range(1, AHEAD)]
    flat = lambda chip, c, h: (chip % chips * 2 + c) * 2 + h
    routes = []
    for i in range(chips):
        routes.append((flat(i, 1, 0), flat(i + 1, 0, 0)))
        routes.append((flat(i, 0, 1), flat(i - AHEAD, 1, 1)))
        routes.append((flat(i, 0, 0), flat(i, 1, 0)))
        routes.append((flat(i, 1, 1), flat(i, 0, 1)))
    rim = lax.ppermute(jnp.where(core == 0, marked[:OWN], marked[OWN:]), ALL, routes)
    routes = []
    for i in range(2 * chips):
        routes.append((2 * i, (2 * i + 2) % (4 * chips)))
        routes.append((2 * i + 1, (2 * i - 1) % (4 * chips)))
    rim_target = lax.ppermute(jnp.where(chan == 0, target[24:], target[:8]), ALL, routes)
    sibling = [swap(value, "core") for value in same]
    keep, give, w = run_kernel(
        scalars, *same, *sibling, rim, packed, other_pack, target, rim_target
    )

    w_mine = jnp.where(core == 0, w[0], w[1])
    w = w_mine + swap(jnp.where(core == 0, w[1], w[0]), "core")
    w = jnp.sum(exchange(w, ("chan",) + CHIPS), axis=0, keepdims=True)
    w = exchange(jnp.broadcast_to(w, (chips, PIECE)), CHIPS)

    given = swap(give, "core").astype(F32)
    total = 0.0
    for n in range(AHEAD):
        before = given[n - 1] if n > 0 else 0.0
        behind = given[n] if n < AHEAD - 1 else 0.0
        block = keep[n] + jnp.where(core == 0, before, behind)
        if n > 0:
            block = cycle(block.astype(BF16), CHIPS, chips, n).astype(F32)
        total = total + block
    mine = jnp.where(chan == 0, total[:, :256], total[:, 256:])
    other = jnp.where(chan == 0, total[:, 256:], total[:, :256])
    mine = mine + swap(other.astype(BF16), "chan").astype(F32)
    proj, pair, head = run_final(scalars, w, swap(w, "core"))
    return mine, proj.T, pair, head


def solution(mesh):
    split = mesh.devices.reshape(2, 4, 8, 2, 2)
    sizes = dict(yl=2, x=4, z=8, core=2, chan=2)
    fine = Mesh(split, ("yl", "x", "z", "core", "chan"))
    return jax.shard_map(
        functools.partial(local, sizes),
        mesh=fine,
        in_specs=(
            P(GENOME, None),
            P(GENOME),
            P(GENOME, None),
            P(None, "chan"),
            P("chan", None),
            P(None, "chan", None),
            P(None, "chan"),
            P(),
        ),
        out_specs=(P(GENOME, "chan"), P(None, "chan"), P(None, "chan", None), P(None, "chan")),
        check_vma=False,
    )
```

```python
import functools

import jax
import jax.numpy as jnp
from jax import lax
from jax.experimental import pallas as pl
from jax.experimental.pallas import tpu as pltpu
from jax.sharding import Mesh, PartitionSpec as P

F32 = jnp.float32
BF16 = jnp.bfloat16
EMB = 512
CH = 64
HALF = CH // 2
BAND = 256
BINS = 4096
BLOCK = 32
OWN = 16
HALO = 16
ROWS = OWN + 2 * HALO
WIDE = 384
LEAD = 32
PACK = 96
MARKED = EMB + 128
PIECE = 384
AHEAD = 5
GENOME = ("yl", "x", "z", "core")
CHIPS = ("yl", "x", "z")
ALL = GENOME + ("chan",)
NT = (((1,), (1,)), ((), ()))
TN = (((0,), (0,)), ((), ()))


def dot(a, b, dims=(((1,), (0,)), ((), ()))):
    return lax.dot_general(a, b, dims, preferred_element_type=F32)


def shift_up(v, by):
    low = lax.broadcasted_iota(jnp.int32, (v.shape[0], 128), 1) < by
    tiles = [pltpu.roll(v[:, t : t + 128], by, 1) for t in range(0, v.shape[1], 128)]
    return jnp.concatenate([jnp.where(low, tiles[n - 1], tiles[n]) for n in range(len(tiles))], 1)


def shift_down(v, by):
    low = lax.broadcasted_iota(jnp.int32, (v.shape[0], 128), 1) < 128 - by
    tiles = [pltpu.roll(v[:, t : t + 128], 128 - by, 1) for t in range(0, v.shape[1], 128)]
    tiles.append(tiles[0])
    return jnp.concatenate(
        [jnp.where(low, tiles[n], tiles[n + 1]) for n in range(len(tiles) - 1)], 1
    )


def silu_and_slope(u, mask):
    t = jnp.tanh(u)
    w = (1.0 + t) * mask
    value = u * w
    return value, w + (value - value * t)


def pack_kernel(emb, mask, proj, bias, pair, head, marked, packed):
    marked[:, :EMB] = emb[...]
    line = jnp.broadcast_to(mask[...].astype(F32), (BLOCK, BLOCK))
    row = lax.broadcasted_iota(jnp.int32, (BLOCK, BLOCK), 0)
    own = jnp.where(row == lax.broadcasted_iota(jnp.int32, (BLOCK, BLOCK), 1), line, 0.0)
    column = jnp.sum(own, axis=1, keepdims=True)
    marked[:, EMB:] = jnp.broadcast_to(column, (BLOCK, 128)).astype(BF16)
    packed[:HALF, :] = proj[...]
    packed[32:48, :] = jnp.concatenate([bias[:16], bias[16:]], 1)
    taps = [pair[tap].astype(F32) for tap in range(9)]
    packed[48:80, :] = jnp.concatenate(taps[:8], 1).astype(BF16)
    last = jnp.concatenate([taps[8][:16], taps[8][16:]], 1)
    heads = jnp.concatenate([head[...].astype(F32), jnp.zeros((7, HALF), F32)], 0)
    rest = jnp.zeros((16, EMB - 128 - HALF), F32)
    packed[80:96, :] = jnp.concatenate([last, heads, rest], 1).astype(BF16)


def kernel(scalars, *refs):
    same, sibling = refs[:AHEAD], refs[AHEAD : 2 * AHEAD]
    (
        rim, own_pack, other_pack, target, rim_target,
        keep_out, give_out, w_out,
        window, wt, bias, kf, kb, hk, hkt,
        et, ef, mrow, cmask, pre, hz, d0, h1, d1, s1, s1b, sz, aown, q, rgb, tgw, pacc, g1, pg, hg, gs,
    ) = refs[2 * AHEAD :]
    r0 = scalars[0]
    r1 = scalars[1]
    w0 = scalars[2]
    core = scalars[3]
    chan = scalars[4]
    col = lax.broadcasted_iota(jnp.int32, (1, WIDE), 1)

    def band(r):
        high = jnp.where(w0 + r >= 0, jnp.minimum(r + BAND, BINS - w0), 0)
        return jnp.where((col >= r) & (col < high), 1.0, 0.0).astype(F32)

    window[...] = jnp.zeros_like(window)
    for n in range(AHEAD):
        at = LEAD + 64 * n + HALO - OWN * chan
        window[pl.ds(pl.multiple_of(at, 16), BLOCK), :] = same[n][...]
        at = at + BLOCK * (1 - 2 * core)
        window[pl.ds(pl.multiple_of(at, 16), BLOCK), :] = sibling[n][...]

    @pl.when((core == 0) & (chan == 0))
    def _():
        window[LEAD : LEAD + OWN, :] = rim[...]

    @pl.when((core == 1) & (chan == 1))
    def _():
        window[LEAD + 288 : LEAD + 304, :] = rim[...]

    win = window.at[LEAD : LEAD + WIDE]

    flip = jnp.full((PACK, EMB), chan, jnp.int32) == 0
    mine, other = own_pack[...].astype(F32), other_pack[...].astype(F32)
    halves = [jnp.where(flip, mine, other), jnp.where(flip, other, mine)]
    wt[...] = jnp.concatenate([h[:HALF] for h in halves], 0)
    rows = []
    for h in halves:
        rows += [h[32:48, :BAND], h[32:48, BAND:]]
    bias[...] = jnp.concatenate(
        [0.5 * jnp.concatenate(rows, 0), jnp.zeros((CH, WIDE - BAND), F32)], 1
    )
    taps = []
    for tap in range(9):
        parts = []
        for h in halves:
            if tap < 8:
                parts.append(h[48:80, tap * CH : tap * CH + CH])
            else:
                parts += [h[80:96, :CH], h[80:96, CH : 2 * CH]]
        taps.append(jnp.concatenate(parts, 0))
    grid = lambda pick: jnp.concatenate(
        [jnp.concatenate([taps[pick(n, m)] for m in range(3)], 1) for n in range(3)], 0
    )
    kf[...] = (0.5 * grid(lambda b, a: 3 * a + b)).astype(BF16)
    kb[...] = (0.5 * grid(lambda a, b: 3 * a + b)).T.astype(BF16)
    heads = jnp.concatenate([h[80:96, 128 : 128 + HALF] for h in halves], 1)
    rest = jnp.zeros((5, CH), F32)
    rows = []
    for b in range(3):
        rows += [heads[3 * a + b : 3 * a + b + 1] for a in range(3)] + [rest]
    hk[...] = jnp.concatenate(rows, 0).astype(BF16)
    rows = []
    for a in range(3):
        rows += [heads[3 * a : 3 * a + 3], rest] * 2
    hkt[...] = (0.5 * jnp.concatenate(rows, 0)).T.astype(BF16)

    wide = win[:, :EMB].astype(F32)
    et[...] = wide.T.astype(BF16)
    ef[...] = wide[:ROWS]
    marks = win[:, EMB:].astype(F32)
    mrow[...] = marks[:ROWS]
    cmask[...] = marks.T[:8]

    tgt = jnp.where(
        jnp.full((BLOCK, BAND), chan, jnp.int32) == 0,
        jnp.concatenate([rim_target[...], target[:24]], 0),
        jnp.concatenate([target[8:], rim_target[...]], 0),
    )
    padded = jnp.concatenate([tgt, jnp.zeros((BLOCK, WIDE - BAND), F32)], 1)
    tgw[...] = pltpu.roll(padded, 8, 1, stride=1, stride_axis=0)

    def forward(b, _):
        e8 = ef[pl.ds(pl.multiple_of(b * 8, 8), 8), :]
        w = 0.5 * wt[...]
        a = jnp.concatenate([(w * e8[k : k + 1]).astype(BF16) for k in range(8)], 0)

        @pl.when((b >= 2) & (b < 4))
        def _():
            aown[pl.ds(pl.multiple_of((b - 2) * 512, 512), 512), :] = a

        pre[...] = dot(a, et[...])

        for k in range(8):
            r = b * 8 + k
            u = pre[k * CH : k * CH + CH, :] + shift_up(bias[...], r)
            value, gain = silu_and_slope(u, band(r))
            hz[r] = value.astype(BF16)
            d0[r] = gain
        return 0

    lax.fori_loop(0, ROWS // 8, forward, 0)

    def near(field, r, step):
        return jnp.concatenate([field[r - step], field[r], field[r + step]], 0)

    def four(rows):
        return jnp.concatenate(rows, 1)

    def part(v, k):
        return v[:, k * WIDE : k * WIDE + WIDE]

    def second(n, _):
        first = 4 + n * 4
        p = dot(kf[...], four([near(hz, first + k, r0) for k in range(4)]))
        ones = []
        for k in range(4):
            r = first + k
            pk = part(p, k)
            u = shift_up(pk[:CH], r0) + pk[CH : 2 * CH] + shift_down(pk[2 * CH :], r0)
            value, gain = silu_and_slope(u, band(r))
            ones.append(value.astype(BF16))
            h1[r] = ones[k]
            d1[r] = gain
        p = dot(hk[...], four(ones))
        for k in range(4):
            pk = part(p, k)
            q[first + k] = shift_up(pk[:8], r1) + pk[8:16] + shift_down(pk[16:24], r1)
        return 0

    lax.fori_loop(0, 10, second, 0)

    which = lax.broadcasted_iota(jnp.int32, (8, WIDE), 0)

    def residual(n, _):
        for k in range(4):
            r = 8 + n * 4 + k
            pred = q[r - r1][0:1] + q[r][1:2] + q[r + r1][2:3]
            mark = mrow[pl.ds(r, 1), :]
            lm = jnp.concatenate([mark] * (WIDE // 128), 1) * cmask[0:1] * band(r)
            rg = lm * (pred - tgw[pl.ds(r - 8, 1), :]) * (1.0 / BAND)
            rg = jnp.broadcast_to(rg, (8, WIDE))
            taps = jnp.where(
                which == 0,
                shift_down(rg, r1),
                jnp.where(which == 1, rg, jnp.where(which == 2, shift_up(rg, r1), 0.0)),
            )
            high = taps.astype(BF16).astype(F32)
            rgb[r] = jnp.concatenate([high, taps - high], 0).astype(BF16)
        return 0

    lax.fori_loop(0, 8, residual, 0)

    def slope(n, _):
        first = 12 + n * 4
        h = dot(hkt[...], four([near(rgb, first + k, -r1) for k in range(4)]))
        for k in range(4):
            r = first + k
            sf = part(h, k) * d1[r]
            s = sf.astype(BF16)
            s1[r] = s
            sf = s.astype(F32)
            s1b[r] = jnp.concatenate(
                [shift_down(sf, r0).astype(BF16), s, shift_up(sf, r0).astype(BF16)], 0
            )
        return 0

    lax.fori_loop(0, 6, slope, 0)

    pg[...] = jnp.zeros_like(pg)
    hg[...] = jnp.zeros_like(hg)

    def grads(n, _):
        first = HALO + n * 4
        rows = [first + k for k in range(4)]
        pg[...] += dot(four([s1b[r] for r in rows]), four([near(hz, r, r0) for r in rows]), NT)
        hg[...] += dot(four([rgb[r] for r in rows]), four([near(h1, r, r1) for r in rows]), NT)
        p = dot(kb[...], four([near(s1, r, -r0) for r in rows]))
        for k in range(4):
            pk = part(p, k)
            zg = shift_down(pk[:CH], r0) + pk[CH : 2 * CH] + shift_up(pk[2 * CH :], r0)
            at = pl.multiple_of((n * 4 + k) * CH, CH)
            sz[pl.ds(at, CH), :] = (zg * d0[first + k]).astype(BF16)
        return 0

    lax.fori_loop(0, 4, grads, 0)

    pacc[...] = jnp.zeros_like(pacc)

    def back(n, _):
        t = dot(sz[pl.ds(pl.multiple_of(n * 256, 256), 256), :], win[:, :EMB])
        w = wt[...]
        acc = pacc[...]
        for k in range(4):
            tr = t[k * CH : (k + 1) * CH]
            g1[pl.ds(n * 4 + k, 1), :] = jnp.sum(w * tr, axis=0, keepdims=True)
            acc = acc + tr * ef[pl.ds(HALO + n * 4 + k, 1), :]
        pacc[...] = acc
        return 0

    lax.fori_loop(0, 4, back, 0)
    g = dot(sz[...], aown[...], TN)
    g = 2.0 * g
    gs[...] = g
    gs[HALO : HALO + OWN, :] = g[HALO : HALO + OWN] + g1[...]
    for n in range(2 * AHEAD - 1):
        block = gs[pl.ds(pl.multiple_of(BLOCK * n + HALO - OWN * chan, 16), BLOCK), :]
        if n % 2:
            give_out[n // 2] = block.astype(BF16)
        else:
            keep_out[n // 2] = block

    heads = hg[0:8] + hg[8:16]
    blank = jnp.zeros((8, 256 - 3 * CH), F32)
    for half in range(2):
        tiles = []
        for a in range(4):
            for b in range(4):
                tiles.append(pacc[half * 32 + a * 8 : half * 32 + a * 8 + 8, b * 128 : b * 128 + 128])
        for b in range(3):
            for a in range(4):
                at = b * CH + half * 32 + a * 8
                row = jnp.concatenate([pg[at : at + 8, :], blank], 1)
                tiles += [row[:, :128], row[:, 128:]]
        row = jnp.concatenate([heads, blank], 1)
        tiles += [row[:, :128], row[:, 128:]]
        tiles += [jnp.zeros((8, 128), F32)] * (48 - len(tiles))
        for t, tile in enumerate(tiles):
            at, lane = half * 64 + t % 24 // 3 * 8, t % 3 * 128
            w_out[t // 24, at : at + 8, lane : lane + 128] = tile


VMEM = pl.BlockSpec(memory_space=pltpu.VMEM)
SMEM = pl.BlockSpec(memory_space=pltpu.SMEM)


def run_pack(*args):
    return pl.pallas_call(
        pack_kernel,
        out_shape=(
            jax.ShapeDtypeStruct((BLOCK, MARKED), BF16),
            jax.ShapeDtypeStruct((PACK, EMB), BF16),
        ),
        in_specs=[VMEM] * len(args),
        out_specs=(VMEM, VMEM),
    )(*args)


def run_kernel(*args):
    return pl.pallas_call(
        kernel,
        out_shape=(
            jax.ShapeDtypeStruct((AHEAD, BLOCK, EMB), F32),
            jax.ShapeDtypeStruct((AHEAD - 1, BLOCK, EMB), BF16),
            jax.ShapeDtypeStruct((2, 128, PIECE), F32),
        ),
        in_specs=[SMEM] + [VMEM] * (len(args) - 1),
        out_specs=(VMEM, VMEM, VMEM),
        scratch_shapes=[
            pltpu.VMEM((LEAD + WIDE, MARKED), BF16),
            pltpu.VMEM((CH, EMB), F32),
            pltpu.VMEM((CH, WIDE), F32),
            pltpu.VMEM((3 * CH, 3 * CH), BF16),
            pltpu.VMEM((3 * CH, 3 * CH), BF16),
            pltpu.VMEM((24, CH), BF16),
            pltpu.VMEM((CH, 48), BF16),
            pltpu.VMEM((EMB, WIDE), BF16),
            pltpu.VMEM((ROWS, EMB), F32),
            pltpu.VMEM((ROWS, 128), F32),
            pltpu.VMEM((8, WIDE), F32),
            pltpu.VMEM((8 * CH, WIDE), F32),
            pltpu.VMEM((ROWS, CH, WIDE), BF16),
            pltpu.VMEM((ROWS, CH, WIDE), F32),
            pltpu.VMEM((ROWS, CH, WIDE), BF16),
            pltpu.VMEM((ROWS, CH, WIDE), F32),
            pltpu.VMEM((ROWS, CH, WIDE), BF16),
            pltpu.VMEM((ROWS, 3 * CH, WIDE), BF16),
            pltpu.VMEM((OWN * CH, WIDE), BF16),
            pltpu.VMEM((OWN * CH, EMB), BF16),
            pltpu.VMEM((ROWS, 8, WIDE), F32),
            pltpu.VMEM((ROWS, 16, WIDE), BF16),
            pltpu.VMEM((BLOCK, WIDE), F32),
            pltpu.VMEM((CH, EMB), F32),
            pltpu.VMEM((OWN, EMB), F32),
            pltpu.VMEM((3 * CH, 3 * CH), F32),
            pltpu.VMEM((16, 3 * CH), F32),
            pltpu.VMEM((WIDE, EMB), F32),
        ],
        compiler_params=pltpu.CompilerParams(vmem_limit_bytes=48 * 1024 * 1024),
    )(*args)


def final_kernel(scalars, own, other, proj_out, pair_out, head_out):
    core = scalars[3]
    chan = scalars[4]
    flip = jnp.full((64, PIECE), core, jnp.int32) == 0
    mine, theirs = own[...], other[...]
    scale = 1.0 / BINS
    both = [jnp.where(flip, mine, theirs) * scale, jnp.where(flip, theirs, mine) * scale]

    def tile(t):
        at, lane = t % 24 // 3 * 8, t % 3 * 128
        return both[t // 24][at : at + 8, lane : lane + 128]

    proj = [jnp.concatenate([tile(4 * a + b) for b in range(4)], 1) for a in range(4)]
    proj_out[...] = jnp.concatenate(proj, 0)
    for b in range(3):
        for a in range(4):
            t = 16 + (b * 4 + a) * 2
            row = jnp.concatenate([tile(t), tile(t + 1)], 1)
            for k in range(3):
                pair_out[3 * k + b, 8 * a : 8 * a + 8, :] = row[:, CH * k : CH * k + CH]
    row = jnp.concatenate([tile(40), tile(41)], 1)
    for k in range(3):
        line = row[:3, CH * k : CH * k + CH]
        first = jnp.full((3, HALF), chan, jnp.int32) == 0
        head_out[3 * k : 3 * k + 3, :] = jnp.where(first, line[:, :HALF], line[:, HALF:])


def run_final(*args):
    return pl.pallas_call(
        final_kernel,
        out_shape=(
            jax.ShapeDtypeStruct((HALF, EMB), F32),
            jax.ShapeDtypeStruct((9, HALF, CH), F32),
            jax.ShapeDtypeStruct((9, HALF), F32),
        ),
        in_specs=[SMEM] + [VMEM] * (len(args) - 1),
        out_specs=(VMEM, VMEM, VMEM),
    )(*args)


def swap(value, axis):
    return lax.ppermute(value, axis, [(0, 1), (1, 0)])


def cycle(value, axes, length, by):
    return lax.ppermute(value, axes, [(i, (i + by) % length) for i in range(length)])


def exchange(value, axes):
    return lax.all_to_all(value, axes, 0, 0, tiled=True)


def local(sizes, embeddings, bin_mask, target, proj_weight, dist_bias, pair_kernel, head_kernel, dilations):
    chips = sizes["yl"] * sizes["x"] * sizes["z"]
    chan = lax.axis_index("chan")
    core = lax.axis_index("core")
    first = (lax.axis_index(GENOME) * 2 + chan) * OWN
    scalars = jnp.stack([dilations[0], dilations[1], first - HALO, core, chan]).astype(jnp.int32)

    marked, packed = run_pack(
        embeddings, bin_mask[None, :], proj_weight.T, dist_bias, pair_kernel, head_kernel
    )
    other_pack = swap(packed, "chan")
    same = [marked] + [cycle(marked, CHIPS, chips, -n) for n in range(1, AHEAD)]
    flat = lambda chip, c, h: (chip % chips * 2 + c) * 2 + h
    routes = []
    for i in range(chips):
        routes.append((flat(i, 1, 0), flat(i + 1, 0, 0)))
        routes.append((flat(i, 0, 1), flat(i - AHEAD, 1, 1)))
        routes.append((flat(i, 0, 0), flat(i, 1, 0)))
        routes.append((flat(i, 1, 1), flat(i, 0, 1)))
    rim = lax.ppermute(jnp.where(core == 0, marked[:OWN], marked[OWN:]), ALL, routes)
    routes = []
    for i in range(2 * chips):
        routes.append((2 * i, (2 * i + 2) % (4 * chips)))
        routes.append((2 * i + 1, (2 * i - 1) % (4 * chips)))
    rim_target = lax.ppermute(jnp.where(chan == 0, target[24:], target[:8]), ALL, routes)
    sibling = [swap(value, "core") for value in same]
    keep, give, w = run_kernel(
        scalars, *same, *sibling, rim, packed, other_pack, target, rim_target
    )

    w_mine = jnp.where(core == 0, w[0], w[1])
    w = w_mine + swap(jnp.where(core == 0, w[1], w[0]), "core")
    w = jnp.sum(exchange(w, ("chan",) + CHIPS), axis=0, keepdims=True)
    w = exchange(jnp.broadcast_to(w, (chips, PIECE)), CHIPS)

    given = swap(give, "core").astype(F32)
    total = 0.0
    for n in range(AHEAD):
        before = given[n - 1] if n > 0 else 0.0
        behind = given[n] if n < AHEAD - 1 else 0.0
        block = keep[n] + jnp.where(core == 0, before, behind)
        if n > 0:
            block = cycle(block.astype(BF16), CHIPS, chips, n).astype(F32)
        total = total + block
    mine = jnp.where(chan == 0, total[:, :256], total[:, 256:])
    other = jnp.where(chan == 0, total[:, 256:], total[:, :256])
    mine = mine + swap(other.astype(BF16), "chan").astype(F32)
    proj, pair, head = run_final(scalars, w, swap(w, "core"))
    return mine, proj.T, pair, head


def solution(mesh):
    split = mesh.devices.reshape(2, 4, 8, 2, 2)
    sizes = dict(yl=2, x=4, z=8, core=2, chan=2)
    fine = Mesh(split, ("yl", "x", "z", "core", "chan"))
    return jax.shard_map(
        functools.partial(local, sizes),
        mesh=fine,
        in_specs=(
            P(GENOME, None),
            P(GENOME),
            P(GENOME, None),
            P(None, "chan"),
            P("chan", None),
            P(None, "chan", None),
            P(None, "chan"),
            P(),
        ),
        out_specs=(P(GENOME, "chan"), P(None, "chan"), P(None, "chan", None), P(None, "chan")),
        check_vma=False,
    )
```

```python
import functools

import jax
import jax.numpy as jnp
from jax import lax
from jax.experimental import pallas as pl
from jax.experimental.pallas import tpu as pltpu
from jax.sharding import Mesh, PartitionSpec as P

F32 = jnp.float32
BF16 = jnp.bfloat16
EMB = 512
CH = 64
HALF = CH // 2
BAND = 256
BINS = 4096
BLOCK = 32
OWN = 16
HALO = 16
ROWS = OWN + 2 * HALO
WIDE = 384
LEAD = 32
PACK = 96
MARKED = EMB + 128
SLOTS = 64
TILES = 21
AHEAD = 5
GENOME = ("yl", "x", "z", "core")
CHIPS = ("yl", "x", "z")
ALL = GENOME + ("chan",)
NT = (((1,), (1,)), ((), ()))
TN = (((0,), (0,)), ((), ()))


def dot(a, b, dims=(((1,), (0,)), ((), ()))):
    return lax.dot_general(a, b, dims, preferred_element_type=F32)


def shift_up(v, by):
    low = lax.broadcasted_iota(jnp.int32, (v.shape[0], 128), 1) < by
    tiles = [pltpu.roll(v[:, t : t + 128], by, 1) for t in range(0, v.shape[1], 128)]
    return jnp.concatenate([jnp.where(low, tiles[n - 1], tiles[n]) for n in range(len(tiles))], 1)


def shift_down(v, by):
    low = lax.broadcasted_iota(jnp.int32, (v.shape[0], 128), 1) < 128 - by
    tiles = [pltpu.roll(v[:, t : t + 128], 128 - by, 1) for t in range(0, v.shape[1], 128)]
    tiles.append(tiles[0])
    return jnp.concatenate(
        [jnp.where(low, tiles[n], tiles[n + 1]) for n in range(len(tiles) - 1)], 1
    )


def silu_and_slope(u, mask):
    t = jnp.tanh(u)
    w = (1.0 + t) * mask
    value = u * w
    return value, w + (value - value * t)


def mark_kernel(place, emb, mask, target, marked, first, rim):
    core = place[1]
    chan = place[2]
    line = jnp.broadcast_to(mask[...].astype(F32), (BLOCK, BLOCK))
    row = lax.broadcasted_iota(jnp.int32, (BLOCK, BLOCK), 0)
    own = jnp.where(row == lax.broadcasted_iota(jnp.int32, (BLOCK, BLOCK), 1), line, 0.0)
    column = jnp.sum(own, axis=1, keepdims=True)
    column = jnp.broadcast_to(column, (BLOCK, 128)).astype(BF16)
    for out in (marked, first):
        out[:, :EMB] = emb[...]
        out[:, EMB:MARKED] = column
    rows = target[pl.ds(pl.multiple_of(24 - 24 * chan, 8), 8), :]
    high = rows.astype(BF16).astype(F32)
    low = rows - high
    high = jnp.concatenate([high[:, :128], high[:, 128:]], 0).astype(BF16)
    low = jnp.concatenate([low[:, :128], low[:, 128:]], 0).astype(BF16)
    first[:OWN, MARKED:] = high
    first[OWN:, MARKED:] = low
    rim[:, :MARKED] = marked[pl.ds(pl.multiple_of(core * OWN, OWN), OWN), :]
    rim[:, MARKED : MARKED + 128] = high
    rim[:, MARKED + 128 :] = low


def pack_kernel(proj, bias, pair, head, packed):
    packed[:HALF, :] = proj[...]
    packed[32:48, :] = jnp.concatenate([bias[:16], bias[16:]], 1)
    taps = [pair[tap].astype(F32) for tap in range(9)]
    packed[48:80, :] = jnp.concatenate(taps[:8], 1).astype(BF16)
    last = jnp.concatenate([taps[8][:16], taps[8][16:]], 1)
    heads = jnp.concatenate([head[...].astype(F32), jnp.zeros((7, HALF), F32)], 0)
    blank = jnp.zeros((16, EMB - 128 - HALF), F32)
    packed[80:96, :] = jnp.concatenate([last, heads, blank], 1).astype(BF16)


def kernel(rates, place, *refs):
    same, sibling = refs[:AHEAD], refs[AHEAD : 2 * AHEAD]
    (
        rim, own_pack, other_pack, target,
        keep_out, give_out, w_out,
        window, wt, bias, kf, kb, hk, hkt,
        ef, mrow, cmask, hz, d0, h1, d1, s1, s1b, sz, aown, q, rgb, tgw, pacc, g1, pg, hg, gs,
    ) = refs[2 * AHEAD :]
    r0 = rates[0]
    r1 = rates[1]
    w0 = place[0]
    core = place[1]
    chan = place[2]
    col = lax.broadcasted_iota(jnp.int32, (1, WIDE), 1)

    def band(r):
        high = jnp.where(w0 + r >= 0, jnp.minimum(r + BAND, BINS - w0), 0)
        return jnp.where((col >= r) & (col < high), 1.0, 0.0).astype(F32)

    window[...] = jnp.zeros_like(window)
    for n in range(AHEAD):
        at = LEAD + 64 * n + HALO - OWN * chan
        window[pl.ds(pl.multiple_of(at, 16), BLOCK), :] = same[n][:, :MARKED]
        at = at + BLOCK * (1 - 2 * core)
        window[pl.ds(pl.multiple_of(at, 16), BLOCK), :] = sibling[n][:, :MARKED]

    @pl.when((core == 0) & (chan == 0))
    def _():
        window[LEAD : LEAD + OWN, :] = rim[:, :MARKED]

    @pl.when((core == 1) & (chan == 1))
    def _():
        window[LEAD + 288 : LEAD + 304, :] = rim[:, :MARKED]

    win = window.at[LEAD : LEAD + WIDE]

    flip = jnp.full((PACK, EMB), chan, jnp.int32) == 0
    mine, other = own_pack[...].astype(F32), other_pack[...].astype(F32)
    halves = [jnp.where(flip, mine, other), jnp.where(flip, other, mine)]
    wt[...] = jnp.concatenate([h[:HALF] for h in halves], 0)
    rows = []
    for h in halves:
        rows += [h[32:48, :BAND], h[32:48, BAND:]]
    bias[...] = jnp.concatenate(
        [0.5 * jnp.concatenate(rows, 0), jnp.zeros((CH, WIDE - BAND), F32)], 1
    )
    taps = []
    for tap in range(9):
        parts = []
        for h in halves:
            if tap < 8:
                parts.append(h[48:80, tap * CH : tap * CH + CH])
            else:
                parts += [h[80:96, :CH], h[80:96, CH : 2 * CH]]
        taps.append(jnp.concatenate(parts, 0))
    grid = lambda pick: jnp.concatenate(
        [jnp.concatenate([taps[pick(n, m)] for m in range(3)], 1) for n in range(3)], 0
    )
    kf[...] = (0.5 * grid(lambda b, a: 3 * a + b)).astype(BF16)
    kb[...] = (0.5 * grid(lambda a, b: 3 * a + b)).T.astype(BF16)
    heads = jnp.concatenate([h[80:96, 128 : 128 + HALF] for h in halves], 1)
    rest = jnp.zeros((5, CH), F32)
    rows = []
    for b in range(3):
        rows += [heads[3 * a + b : 3 * a + b + 1] for a in range(3)] + [rest]
    hk[...] = jnp.concatenate(rows, 0).astype(BF16)
    rows = []
    for a in range(3):
        rows += [heads[3 * a : 3 * a + 3], rest] * 2
    hkt[...] = (0.5 * jnp.concatenate(rows, 0)).T.astype(BF16)

    wide = win[:, :EMB].astype(F32)
    ef[...] = wide[:ROWS]
    marks = win[:, EMB:].astype(F32)
    mrow[...] = marks[:ROWS]
    cmask[...] = marks.T[:8]

    def joined(parts):
        whole = parts[0].astype(F32) + parts[1].astype(F32)
        return jnp.concatenate([whole[:8], whole[8:]], 1)

    def sent(ref):
        return joined([ref[:OWN, MARKED:], ref[OWN:, MARKED:]])

    def at_core(zero, one):
        return jnp.where(jnp.full((8, BAND), core, jnp.int32) == 0, zero, one)

    before = joined([rim[:, MARKED : MARKED + 128], rim[:, MARKED + 128 :]])
    before = at_core(before, sent(sibling[0]))
    behind = at_core(sent(sibling[0]), sent(sibling[1]))
    tgt = jnp.where(
        jnp.full((BLOCK, BAND), chan, jnp.int32) == 0,
        jnp.concatenate([before, target[:24]], 0),
        jnp.concatenate([target[8:], behind], 0),
    )
    padded = jnp.concatenate([tgt, jnp.zeros((BLOCK, WIDE - BAND), F32)], 1)
    tgw[...] = pltpu.roll(padded, 8, 1, stride=1, stride_axis=0)

    for b in range(ROWS // 8):
        e8 = ef[b * 8 : b * 8 + 8, :]
        w = 0.5 * wt[...]
        a = jnp.concatenate([(w * e8[k : k + 1]).astype(BF16) for k in range(8)], 0)
        if 2 <= b < 4:
            aown[(b - 2) * 512 : (b - 1) * 512, :] = a
        p = dot(a, win[:, :EMB], NT)
        for k in range(8):
            r = b * 8 + k
            u = p[k * CH : k * CH + CH, :] + shift_up(bias[...], r)
            value, gain = silu_and_slope(u, band(r))
            hz[r] = value.astype(BF16)
            d0[r] = gain

    def near(field, r, step):
        return jnp.concatenate([field[r - step], field[r], field[r + step]], 0)

    def side(rows):
        return jnp.concatenate(rows, 1)

    def part(v, k):
        return v[:, k * WIDE : k * WIDE + WIDE]

    def second(n, _):
        first = 4 + n * 20
        p = dot(kf[...], side([near(hz, first + k, r0) for k in range(20)]))
        ones = []
        for k in range(20):
            r = first + k
            pk = part(p, k)
            u = shift_up(pk[:CH], r0) + pk[CH : 2 * CH] + shift_down(pk[2 * CH :], r0)
            value, gain = silu_and_slope(u, band(r))
            ones.append(value.astype(BF16))
            h1[r] = ones[k]
            d1[r] = gain
        p = dot(hk[...], side(ones))
        for k in range(20):
            pk = part(p, k)
            q[first + k] = shift_up(pk[:8], r1) + pk[8:16] + shift_down(pk[16:24], r1)
        return 0

    lax.fori_loop(0, 2, second, 0)

    which = lax.broadcasted_iota(jnp.int32, (8, WIDE), 0)

    def residual(n, _):
        for k in range(16):
            r = 8 + n * 16 + k
            pred = q[r - r1][0:1] + q[r][1:2] + q[r + r1][2:3]
            mark = mrow[pl.ds(r, 1), :]
            lm = jnp.concatenate([mark] * (WIDE // 128), 1) * cmask[0:1] * band(r)
            rg = lm * (pred - tgw[pl.ds(r - 8, 1), :]) * (1.0 / BAND)
            rg = jnp.broadcast_to(rg, (8, WIDE))
            taps = jnp.where(
                which == 0,
                shift_down(rg, r1),
                jnp.where(which == 1, rg, jnp.where(which == 2, shift_up(rg, r1), 0.0)),
            )
            high = taps.astype(BF16).astype(F32)
            rgb[r] = jnp.concatenate([high, taps - high], 0).astype(BF16)
        return 0

    lax.fori_loop(0, 2, residual, 0)

    def slope(n, _):
        first = 12 + n * 24
        h = dot(hkt[...], side([near(rgb, first + k, -r1) for k in range(24)]))
        for k in range(24):
            r = first + k
            sf = part(h, k) * d1[r]
            s = sf.astype(BF16)
            s1[r] = s
            sf = s.astype(F32)
            s1b[r] = jnp.concatenate(
                [shift_down(sf, r0).astype(BF16), s, shift_up(sf, r0).astype(BF16)], 0
            )
        return 0

    lax.fori_loop(0, 1, slope, 0)

    rows = range(HALO, HALO + OWN)
    pg[...] = dot(side([s1b[r] for r in rows]), side([near(hz, r, r0) for r in rows]), NT)
    hg[...] = dot(side([rgb[r] for r in rows]), side([near(h1, r, r1) for r in rows]), NT)
    p = dot(kb[...], side([near(s1, r, -r0) for r in rows]))
    for k, r in enumerate(rows):
        pk = part(p, k)
        zg = shift_down(pk[:CH], r0) + pk[CH : 2 * CH] + shift_up(pk[2 * CH :], r0)
        sz[k * CH : k * CH + CH, :] = (zg * d0[r]).astype(BF16)

    pacc[...] = jnp.zeros_like(pacc)

    w = wt[...]
    for n in range(4):
        t = dot(sz[n * 256 : n * 256 + 256, :], win[:, :EMB])
        for k in range(4):
            i = n * 4 + k
            tr = t[k * CH : (k + 1) * CH]
            g1[i : i + 1, :] = jnp.sum(w * tr, axis=0, keepdims=True)
            pacc[...] += tr * ef[HALO + i : HALO + i + 1, :]
    g = dot(sz[...], aown[...], TN)
    g = 2.0 * g
    gs[...] = g
    gs[HALO : HALO + OWN, :] = g[HALO : HALO + OWN] + g1[...]
    for n in range(2 * AHEAD - 1):
        block = gs[pl.ds(pl.multiple_of(BLOCK * n + HALO - OWN * chan, 16), BLOCK), :]
        if n % 2:
            give_out[n // 2] = block.astype(BF16)
        else:
            keep_out[n // 2] = block

    heads = hg[0:8] + hg[8:16]
    blank = jnp.zeros((8, 256 - 3 * CH), F32)
    for half in range(2):
        tiles = []
        for a in range(4):
            for b in range(4):
                tiles.append(pacc[half * 32 + a * 8 : half * 32 + a * 8 + 8, b * 128 : b * 128 + 128])
        for b in range(3):
            for a in range(4):
                at = b * CH + half * 32 + a * 8
                row = jnp.concatenate([pg[at : at + 8, :], blank], 1)
                tiles += [row[:, :128], row[:, 128:]]
        row = jnp.concatenate([heads, blank], 1)
        tiles += [row[:, :128], row[:, 128:]]
        for t, tile in enumerate(tiles):
            at = half * SLOTS + t % TILES * 2
            w_out[t // TILES, at] = tile[:4]
            w_out[t // TILES, at + 1] = tile[4:]
        for t in range(2):
            at = half * SLOTS + 2 * TILES
            w_out[t, at : at + SLOTS - 2 * TILES] = jnp.zeros((SLOTS - 2 * TILES, 4, 128), F32)


VMEM = pl.BlockSpec(memory_space=pltpu.VMEM)
SMEM = pl.BlockSpec(memory_space=pltpu.SMEM)


def run_mark(place, *args):
    return pl.pallas_call(
        mark_kernel,
        out_shape=(
            jax.ShapeDtypeStruct((BLOCK, MARKED), BF16),
            jax.ShapeDtypeStruct((BLOCK, MARKED + 128), BF16),
            jax.ShapeDtypeStruct((OWN, MARKED + 256), BF16),
        ),
        in_specs=[SMEM] + [VMEM] * len(args),
        out_specs=(VMEM,) * 3,
        compiler_params=pltpu.CompilerParams(vmem_limit_bytes=8 * 1024 * 1024),
    )(place, *args)


def run_pack(*args):
    return pl.pallas_call(
        pack_kernel,
        out_shape=jax.ShapeDtypeStruct((PACK, EMB), BF16),
        in_specs=[VMEM] * len(args),
        out_specs=VMEM,
        compiler_params=pltpu.CompilerParams(vmem_limit_bytes=8 * 1024 * 1024),
    )(*args)


def run_kernel(*args):
    return pl.pallas_call(
        kernel,
        out_shape=(
            jax.ShapeDtypeStruct((AHEAD, BLOCK, EMB), F32),
            jax.ShapeDtypeStruct((AHEAD - 1, BLOCK, EMB), BF16),
            jax.ShapeDtypeStruct((2, 2 * SLOTS, 4, 128), F32),
        ),
        in_specs=[SMEM] * 2 + [VMEM] * (len(args) - 2),
        out_specs=(VMEM, VMEM, VMEM),
        scratch_shapes=[
            pltpu.VMEM((LEAD + WIDE, MARKED), BF16),
            pltpu.VMEM((CH, EMB), F32),
            pltpu.VMEM((CH, WIDE), F32),
            pltpu.VMEM((3 * CH, 3 * CH), BF16),
            pltpu.VMEM((3 * CH, 3 * CH), BF16),
            pltpu.VMEM((24, CH), BF16),
            pltpu.VMEM((CH, 48), BF16),
            pltpu.VMEM((ROWS, EMB), F32),
            pltpu.VMEM((ROWS, 128), F32),
            pltpu.VMEM((8, WIDE), F32),
            pltpu.VMEM((ROWS, CH, WIDE), BF16),
            pltpu.VMEM((ROWS, CH, WIDE), F32),
            pltpu.VMEM((ROWS, CH, WIDE), BF16),
            pltpu.VMEM((ROWS, CH, WIDE), F32),
            pltpu.VMEM((ROWS, CH, WIDE), BF16),
            pltpu.VMEM((ROWS, 3 * CH, WIDE), BF16),
            pltpu.VMEM((OWN * CH, WIDE), BF16),
            pltpu.VMEM((OWN * CH, EMB), BF16),
            pltpu.VMEM((ROWS, 8, WIDE), F32),
            pltpu.VMEM((ROWS, 16, WIDE), BF16),
            pltpu.VMEM((BLOCK, WIDE), F32),
            pltpu.VMEM((CH, EMB), F32),
            pltpu.VMEM((OWN, EMB), F32),
            pltpu.VMEM((3 * CH, 3 * CH), F32),
            pltpu.VMEM((16, 3 * CH), F32),
            pltpu.VMEM((WIDE, EMB), F32),
        ],
        compiler_params=pltpu.CompilerParams(vmem_limit_bytes=48 * 1024 * 1024),
    )(*args)


def final_kernel(place, own, other, *refs):
    *moved, proj_out, pair_out, head_out, emb_out = refs
    total = moved[0][...]
    for block in moved[1:]:
        total = total + block[...].astype(F32)
    emb_out[...] = total
    core = place[1]
    chan = place[2]
    flip = jnp.full((8, 128), core, jnp.int32) == 0
    scale = 1.0 / BINS

    def tile(t):
        at = t % TILES * 2
        mine = jnp.concatenate([own[at], own[at + 1]], 0)
        theirs = jnp.concatenate([other[at], other[at + 1]], 0)
        if t < TILES:
            return jnp.where(flip, mine, theirs) * scale
        return jnp.where(flip, theirs, mine) * scale

    proj = [jnp.concatenate([tile(4 * a + b) for b in range(4)], 1) for a in range(4)]
    proj_out[...] = jnp.concatenate(proj, 0)
    for b in range(3):
        for a in range(4):
            t = 16 + (b * 4 + a) * 2
            row = jnp.concatenate([tile(t), tile(t + 1)], 1)
            for k in range(3):
                pair_out[3 * k + b, 8 * a : 8 * a + 8, :] = row[:, CH * k : CH * k + CH]
    row = jnp.concatenate([tile(40), tile(41)], 1)
    for k in range(3):
        line = row[:3, CH * k : CH * k + CH]
        first = jnp.full((3, HALF), chan, jnp.int32) == 0
        head_out[3 * k : 3 * k + 3, :] = jnp.where(first, line[:, :HALF], line[:, HALF:])


def run_final(*args):
    return pl.pallas_call(
        final_kernel,
        out_shape=(
            jax.ShapeDtypeStruct((HALF, EMB), F32),
            jax.ShapeDtypeStruct((9, HALF, CH), F32),
            jax.ShapeDtypeStruct((9, HALF), F32),
            jax.ShapeDtypeStruct((BLOCK, EMB // 2), F32),
        ),
        in_specs=[SMEM] + [VMEM] * (len(args) - 1),
        out_specs=(VMEM,) * 4,
        compiler_params=pltpu.CompilerParams(vmem_limit_bytes=8 * 1024 * 1024),
    )(*args)


def swap(value, axis):
    return lax.ppermute(value, axis, [(0, 1), (1, 0)])


def cycle(value, axes, length, by):
    return lax.ppermute(value, axes, [(i, (i + by) % length) for i in range(length)])


def exchange(value, axes):
    return lax.all_to_all(value, axes, 0, 0, tiled=True)


def local(sizes, embeddings, bin_mask, target, proj_weight, dist_bias, pair_kernel, head_kernel, dilations):
    chips = sizes["yl"] * sizes["x"] * sizes["z"]
    chan = lax.axis_index("chan")
    core = lax.axis_index("core")
    at = (lax.axis_index(GENOME) * 2 + chan) * OWN - HALO
    place = jnp.stack([at, core, chan]).astype(jnp.int32)

    marked, first, rim = run_mark(place, embeddings, bin_mask[None, :], target)
    packed = run_pack(proj_weight.T, dist_bias, pair_kernel, head_kernel)
    other_pack = swap(packed, "chan")
    same = [first, cycle(first, CHIPS, chips, -1), cycle(marked, CHIPS, chips, -2)]
    same += [cycle(same[n], CHIPS, chips, -2) for n in (1, 2)]
    flat = lambda chip, c, h: (chip % chips * 2 + c) * 2 + h
    routes = []
    for i in range(chips):
        routes.append((flat(i, 1, 0), flat(i + 1, 0, 0)))
        routes.append((flat(i, 0, 1), flat(i - AHEAD, 1, 1)))
        routes.append((flat(i, 0, 0), flat(i, 1, 0)))
        routes.append((flat(i, 1, 1), flat(i, 0, 1)))
    rim = lax.ppermute(rim, ALL, routes)
    sibling = [swap(value, "core") for value in same]
    keep, give, w = run_kernel(
        dilations, place, *same, *sibling, rim, packed, other_pack, target
    )

    given = swap(give, "core").astype(F32)
    none = jnp.zeros((1, BLOCK, EMB), F32)
    before = jnp.concatenate([none, given], 0)
    behind = jnp.concatenate([given, none], 0)
    blocks = keep + jnp.where(core == 0, before, behind)
    low, high = blocks[..., : EMB // 2], blocks[..., EMB // 2 :]
    other = swap(jnp.where(chan == 0, high, low).astype(BF16), "chan")
    blocks = jnp.where(chan == 0, low, high) + other.astype(F32)
    moved = [blocks[0]]
    moved += [cycle(blocks[n].astype(BF16), CHIPS, chips, n) for n in range(1, AHEAD)]

    w = jnp.where(core == 0, w[0], w[1]) + swap(jnp.where(core == 0, w[1], w[0]), "core")
    per = SLOTS // chips
    w = exchange(w.reshape(2 * chips, per * 4, 128), ("chan",) + CHIPS)
    w = jnp.sum(w, axis=0, keepdims=True)
    w, *moved[3:] = lax.optimization_barrier((w, *moved[3:]))
    w = exchange(jnp.broadcast_to(w, (chips, per * 4, 128)), CHIPS).reshape(SLOTS, 4, 128)
    proj, pair, head, emb = run_final(place, w, swap(w, "core"), *moved)
    return emb, proj.T, pair, head


def solution(mesh):
    split = mesh.devices.reshape(2, 4, 8, 2, 2)
    sizes = dict(yl=2, x=4, z=8, core=2, chan=2)
    fine = Mesh(split, ("yl", "x", "z", "core", "chan"))
    return jax.shard_map(
        functools.partial(local, sizes),
        mesh=fine,
        in_specs=(
            P(GENOME, None),
            P(GENOME),
            P(GENOME, None),
            P(None, "chan"),
            P("chan", None),
            P(None, "chan", None),
            P(None, "chan"),
            P(),
        ),
        out_specs=(P(GENOME, "chan"), P(None, "chan"), P(None, "chan", None), P(None, "chan")),
        check_vma=False,
    )
```

```python
import functools

import jax
import jax.numpy as jnp
from jax import lax
from jax.experimental import pallas as pl
from jax.experimental.pallas import tpu as pltpu
from jax.sharding import Mesh, PartitionSpec as P

F32 = jnp.float32
BF16 = jnp.bfloat16
EMB = 512
CH = 64
HALF = CH // 2
BAND = 256
BINS = 4096
BLOCK = 32
OWN = 16
HALO = 16
ROWS = OWN + 2 * HALO
WIDE = 384
LEAD = 32
PACK = 96
MARKED = EMB + 128
SLOTS = 8
TILES = 21
AHEAD = 5
GENOME = ("yl", "x", "z", "core")
CHIPS = ("yl", "x", "z")
ALL = GENOME + ("chan",)
NT = (((1,), (1,)), ((), ()))
TN = (((0,), (0,)), ((), ()))


def dot(a, b, dims=(((1,), (0,)), ((), ()))):
    return lax.dot_general(a, b, dims, preferred_element_type=F32)


def shift_up(v, by):
    low = lax.broadcasted_iota(jnp.int32, (v.shape[0], 128), 1) < by
    tiles = [pltpu.roll(v[:, t : t + 128], by, 1) for t in range(0, v.shape[1], 128)]
    return jnp.concatenate([jnp.where(low, tiles[n - 1], tiles[n]) for n in range(len(tiles))], 1)


def shift_down(v, by):
    low = lax.broadcasted_iota(jnp.int32, (v.shape[0], 128), 1) < 128 - by
    tiles = [pltpu.roll(v[:, t : t + 128], 128 - by, 1) for t in range(0, v.shape[1], 128)]
    tiles.append(tiles[0])
    return jnp.concatenate(
        [jnp.where(low, tiles[n], tiles[n + 1]) for n in range(len(tiles) - 1)], 1
    )


def silu_and_slope(u, mask):
    t = jnp.tanh(u)
    w = (1.0 + t) * mask
    value = u * w
    return value, w + (value - value * t)


def mark_kernel(place, emb, mask, target, marked, first, rim):
    core = place[1]
    chan = place[2]
    line = jnp.broadcast_to(mask[...].astype(F32), (BLOCK, BLOCK))
    row = lax.broadcasted_iota(jnp.int32, (BLOCK, BLOCK), 0)
    own = jnp.where(row == lax.broadcasted_iota(jnp.int32, (BLOCK, BLOCK), 1), line, 0.0)
    column = jnp.sum(own, axis=1, keepdims=True)
    column = jnp.broadcast_to(column, (BLOCK, 128)).astype(BF16)
    for out in (marked, first):
        out[:, :EMB] = emb[...]
        out[:, EMB:MARKED] = column
    rows = target[pl.ds(pl.multiple_of(24 - 24 * chan, 8), 8), :]
    high = rows.astype(BF16).astype(F32)
    low = rows - high
    high = jnp.concatenate([high[:, :128], high[:, 128:]], 0).astype(BF16)
    low = jnp.concatenate([low[:, :128], low[:, 128:]], 0).astype(BF16)
    first[:OWN, MARKED:] = high
    first[OWN:, MARKED:] = low
    rim[:, :MARKED] = marked[pl.ds(pl.multiple_of(core * OWN, OWN), OWN), :]
    rim[:, MARKED : MARKED + 128] = high
    rim[:, MARKED + 128 :] = low


def pack_kernel(proj, bias, pair, head, packed):
    packed[:HALF, :] = proj[...]
    packed[32:48, :] = jnp.concatenate([bias[:16], bias[16:]], 1)
    taps = [pair[tap].astype(F32) for tap in range(9)]
    packed[48:80, :] = jnp.concatenate(taps[:8], 1).astype(BF16)
    last = jnp.concatenate([taps[8][:16], taps[8][16:]], 1)
    heads = jnp.concatenate([head[...].astype(F32), jnp.zeros((7, HALF), F32)], 0)
    blank = jnp.zeros((16, EMB - 128 - HALF), F32)
    packed[80:96, :] = jnp.concatenate([last, heads, blank], 1).astype(BF16)


def kernel(rates, place, *refs):
    same, sibling = refs[:AHEAD], refs[AHEAD : 2 * AHEAD]
    (
        rim, own_pack, other_pack, target,
        keep_out, give_out, w_out,
        window, wt, bias, kf, kb, hk, hkt,
        ef, mrow, cmask, hz, d0, h1, d1, s1, s1b, sz, aown, q, rgb, tgw, pacc, g1, pg, hg, gs,
    ) = refs[2 * AHEAD :]
    r0 = rates[0]
    r1 = rates[1]
    w0 = place[0]
    core = place[1]
    chan = place[2]
    col = lax.broadcasted_iota(jnp.int32, (1, WIDE), 1)

    def band(r):
        high = jnp.where(w0 + r >= 0, jnp.minimum(r + BAND, BINS - w0), 0)
        return jnp.where((col >= r) & (col < high), 1.0, 0.0).astype(F32)

    window[...] = jnp.zeros_like(window)
    for n in range(AHEAD):
        at = LEAD + 64 * n + HALO - OWN * chan
        window[pl.ds(pl.multiple_of(at, 16), BLOCK), :] = same[n][:, :MARKED]
        at = at + BLOCK * (1 - 2 * core)
        window[pl.ds(pl.multiple_of(at, 16), BLOCK), :] = sibling[n][:, :MARKED]

    @pl.when((core == 0) & (chan == 0))
    def _():
        window[LEAD : LEAD + OWN, :] = rim[:, :MARKED]

    @pl.when((core == 1) & (chan == 1))
    def _():
        window[LEAD + 288 : LEAD + 304, :] = rim[:, :MARKED]

    win = window.at[LEAD : LEAD + WIDE]

    flip = jnp.full((PACK, EMB), chan, jnp.int32) == 0
    mine, other = own_pack[...].astype(F32), other_pack[...].astype(F32)
    halves = [jnp.where(flip, mine, other), jnp.where(flip, other, mine)]
    wt[...] = jnp.concatenate([h[:HALF] for h in halves], 0)
    rows = []
    for h in halves:
        rows += [h[32:48, :BAND], h[32:48, BAND:]]
    bias[...] = jnp.concatenate(
        [0.5 * jnp.concatenate(rows, 0), jnp.zeros((CH, WIDE - BAND), F32)], 1
    )
    taps = []
    for tap in range(9):
        parts = []
        for h in halves:
            if tap < 8:
                parts.append(h[48:80, tap * CH : tap * CH + CH])
            else:
                parts += [h[80:96, :CH], h[80:96, CH : 2 * CH]]
        taps.append(jnp.concatenate(parts, 0))
    grid = lambda pick: jnp.concatenate(
        [jnp.concatenate([taps[pick(n, m)] for m in range(3)], 1) for n in range(3)], 0
    )
    kf[...] = (0.5 * grid(lambda b, a: 3 * a + b)).astype(BF16)
    kb[...] = (0.5 * grid(lambda a, b: 3 * a + b)).T.astype(BF16)
    heads = jnp.concatenate([h[80:96, 128 : 128 + HALF] for h in halves], 1)
    rest = jnp.zeros((5, CH), F32)
    rows = []
    for b in range(3):
        rows += [heads[3 * a + b : 3 * a + b + 1] for a in range(3)] + [rest]
    hk[...] = jnp.concatenate(rows, 0).astype(BF16)
    rows = []
    for a in range(3):
        rows += [heads[3 * a : 3 * a + 3], rest] * 2
    hkt[...] = (0.5 * jnp.concatenate(rows, 0)).T.astype(BF16)

    wide = win[:, :EMB].astype(F32)
    ef[...] = wide[:ROWS]
    marks = win[:, EMB:].astype(F32)
    mrow[...] = marks[:ROWS]
    cmask[...] = marks.T[:8]

    def joined(parts):
        whole = parts[0].astype(F32) + parts[1].astype(F32)
        return jnp.concatenate([whole[:8], whole[8:]], 1)

    def sent(ref):
        return joined([ref[:OWN, MARKED:], ref[OWN:, MARKED:]])

    def at_core(zero, one):
        return jnp.where(jnp.full((8, BAND), core, jnp.int32) == 0, zero, one)

    before = joined([rim[:, MARKED : MARKED + 128], rim[:, MARKED + 128 :]])
    before = at_core(before, sent(sibling[0]))
    behind = at_core(sent(sibling[0]), sent(sibling[1]))
    tgt = jnp.where(
        jnp.full((BLOCK, BAND), chan, jnp.int32) == 0,
        jnp.concatenate([before, target[:24]], 0),
        jnp.concatenate([target[8:], behind], 0),
    )
    padded = jnp.concatenate([tgt, jnp.zeros((BLOCK, WIDE - BAND), F32)], 1)
    tgw[...] = pltpu.roll(padded, 8, 1, stride=1, stride_axis=0)

    for b in range(ROWS // 8):
        e8 = ef[b * 8 : b * 8 + 8, :]
        w = 0.5 * wt[...]
        a = jnp.concatenate([(w * e8[k : k + 1]).astype(BF16) for k in range(8)], 0)
        if 2 <= b < 4:
            aown[(b - 2) * 512 : (b - 1) * 512, :] = a
        p = dot(a, win[:, :EMB], NT)
        for k in range(8):
            r = b * 8 + k
            u = p[k * CH : k * CH + CH, :] + shift_up(bias[...], r)
            value, gain = silu_and_slope(u, band(r))
            hz[r] = value.astype(BF16)
            d0[r] = gain

    def near(field, r, step):
        return jnp.concatenate([field[r - step], field[r], field[r + step]], 0)

    def side(rows):
        return jnp.concatenate(rows, 1)

    def part(v, k):
        return v[:, k * WIDE : k * WIDE + WIDE]

    def second(n, _):
        first = 4 + n * 20
        p = dot(kf[...], side([near(hz, first + k, r0) for k in range(20)]))
        ones = []
        for k in range(20):
            r = first + k
            pk = part(p, k)
            u = shift_up(pk[:CH], r0) + pk[CH : 2 * CH] + shift_down(pk[2 * CH :], r0)
            value, gain = silu_and_slope(u, band(r))
            ones.append(value.astype(BF16))
            h1[r] = ones[k]
            d1[r] = gain
        p = dot(hk[...], side(ones))
        for k in range(20):
            pk = part(p, k)
            q[first + k] = shift_up(pk[:8], r1) + pk[8:16] + shift_down(pk[16:24], r1)
        return 0

    lax.fori_loop(0, 2, second, 0)

    which = lax.broadcasted_iota(jnp.int32, (8, WIDE), 0)

    def residual(n, _):
        for k in range(16):
            r = 8 + n * 16 + k
            pred = q[r - r1][0:1] + q[r][1:2] + q[r + r1][2:3]
            mark = mrow[pl.ds(r, 1), :]
            lm = jnp.concatenate([mark] * (WIDE // 128), 1) * cmask[0:1] * band(r)
            rg = lm * (pred - tgw[pl.ds(r - 8, 1), :]) * (1.0 / BAND)
            rg = jnp.broadcast_to(rg, (8, WIDE))
            taps = jnp.where(
                which == 0,
                shift_down(rg, r1),
                jnp.where(which == 1, rg, jnp.where(which == 2, shift_up(rg, r1), 0.0)),
            )
            high = taps.astype(BF16).astype(F32)
            rgb[r] = jnp.concatenate([high, taps - high], 0).astype(BF16)
        return 0

    lax.fori_loop(0, 2, residual, 0)

    def slope(n, _):
        first = 12 + n * 24
        h = dot(hkt[...], side([near(rgb, first + k, -r1) for k in range(24)]))
        for k in range(24):
            r = first + k
            sf = part(h, k) * d1[r]
            s = sf.astype(BF16)
            s1[r] = s
            sf = s.astype(F32)
            s1b[r] = jnp.concatenate(
                [shift_down(sf, r0).astype(BF16), s, shift_up(sf, r0).astype(BF16)], 0
            )
        return 0

    lax.fori_loop(0, 1, slope, 0)

    rows = range(HALO, HALO + OWN)
    pg[...] = dot(side([s1b[r] for r in rows]), side([near(hz, r, r0) for r in rows]), NT)
    hg[...] = dot(side([rgb[r] for r in rows]), side([near(h1, r, r1) for r in rows]), NT)
    p = dot(kb[...], side([near(s1, r, -r0) for r in rows]))
    for k, r in enumerate(rows):
        pk = part(p, k)
        zg = shift_down(pk[:CH], r0) + pk[CH : 2 * CH] + shift_up(pk[2 * CH :], r0)
        sz[k * CH : k * CH + CH, :] = (zg * d0[r]).astype(BF16)

    pacc[...] = jnp.zeros_like(pacc)

    w = wt[...]
    for n in range(4):
        t = dot(sz[n * 256 : n * 256 + 256, :], win[:, :EMB])
        for k in range(4):
            i = n * 4 + k
            tr = t[k * CH : (k + 1) * CH]
            g1[i : i + 1, :] = jnp.sum(w * tr, axis=0, keepdims=True)
            pacc[...] += tr * ef[HALO + i : HALO + i + 1, :]
    g = dot(sz[...], aown[...], TN)
    g = 2.0 * g
    gs[...] = g
    gs[HALO : HALO + OWN, :] = g[HALO : HALO + OWN] + g1[...]
    for n in range(2 * AHEAD - 1):
        block = gs[pl.ds(pl.multiple_of(BLOCK * n + HALO - OWN * chan, 16), BLOCK), :]
        if n % 2:
            give_out[n // 2] = block.astype(BF16)
        else:
            keep_out[n // 2] = block

    heads = hg[0:8] + hg[8:16]
    blank = jnp.zeros((8, 256 - 3 * CH), F32)
    for half in range(2):
        tiles = []
        for a in range(4):
            for b in range(4):
                tiles.append(pacc[half * 32 + a * 8 : half * 32 + a * 8 + 8, b * 128 : b * 128 + 128])
        for b in range(3):
            for a in range(4):
                at = b * CH + half * 32 + a * 8
                row = jnp.concatenate([pg[at : at + 8, :], blank], 1)
                tiles += [row[:, :128], row[:, 128:]]
        row = jnp.concatenate([heads, blank], 1)
        tiles += [row[:, :128], row[:, 128:]]
        for t, tile in enumerate(tiles):
            at, row = half * SLOTS + t % TILES // 3, t % 3 * 8
            w_out[t // TILES, at, row : row + 8, :] = tile
        for t in range(2):
            w_out[t, half * SLOTS + SLOTS - 1] = jnp.zeros((24, 128), F32)


VMEM = pl.BlockSpec(memory_space=pltpu.VMEM)
SMEM = pl.BlockSpec(memory_space=pltpu.SMEM)


def run_mark(place, *args):
    return pl.pallas_call(
        mark_kernel,
        out_shape=(
            jax.ShapeDtypeStruct((BLOCK, MARKED), BF16),
            jax.ShapeDtypeStruct((BLOCK, MARKED + 128), BF16),
            jax.ShapeDtypeStruct((OWN, MARKED + 256), BF16),
        ),
        in_specs=[SMEM] + [VMEM] * len(args),
        out_specs=(VMEM,) * 3,
        compiler_params=pltpu.CompilerParams(vmem_limit_bytes=8 * 1024 * 1024),
    )(place, *args)


def run_pack(*args):
    return pl.pallas_call(
        pack_kernel,
        out_shape=jax.ShapeDtypeStruct((PACK, EMB), BF16),
        in_specs=[VMEM] * len(args),
        out_specs=VMEM,
        compiler_params=pltpu.CompilerParams(vmem_limit_bytes=8 * 1024 * 1024),
    )(*args)


def run_kernel(*args):
    return pl.pallas_call(
        kernel,
        out_shape=(
            jax.ShapeDtypeStruct((AHEAD, BLOCK, EMB), F32),
            jax.ShapeDtypeStruct((AHEAD - 1, BLOCK, EMB), BF16),
            jax.ShapeDtypeStruct((2, 2 * SLOTS, 24, 128), F32),
        ),
        in_specs=[SMEM] * 2 + [VMEM] * (len(args) - 2),
        out_specs=(VMEM, VMEM, VMEM),
        scratch_shapes=[
            pltpu.VMEM((LEAD + WIDE, MARKED), BF16),
            pltpu.VMEM((CH, EMB), F32),
            pltpu.VMEM((CH, WIDE), F32),
            pltpu.VMEM((3 * CH, 3 * CH), BF16),
            pltpu.VMEM((3 * CH, 3 * CH), BF16),
            pltpu.VMEM((24, CH), BF16),
            pltpu.VMEM((CH, 48), BF16),
            pltpu.VMEM((ROWS, EMB), F32),
            pltpu.VMEM((ROWS, 128), F32),
            pltpu.VMEM((8, WIDE), F32),
            pltpu.VMEM((ROWS, CH, WIDE), BF16),
            pltpu.VMEM((ROWS, CH, WIDE), F32),
            pltpu.VMEM((ROWS, CH, WIDE), BF16),
            pltpu.VMEM((ROWS, CH, WIDE), F32),
            pltpu.VMEM((ROWS, CH, WIDE), BF16),
            pltpu.VMEM((ROWS, 3 * CH, WIDE), BF16),
            pltpu.VMEM((OWN * CH, WIDE), BF16),
            pltpu.VMEM((OWN * CH, EMB), BF16),
            pltpu.VMEM((ROWS, 8, WIDE), F32),
            pltpu.VMEM((ROWS, 16, WIDE), BF16),
            pltpu.VMEM((BLOCK, WIDE), F32),
            pltpu.VMEM((CH, EMB), F32),
            pltpu.VMEM((OWN, EMB), F32),
            pltpu.VMEM((3 * CH, 3 * CH), F32),
            pltpu.VMEM((16, 3 * CH), F32),
            pltpu.VMEM((WIDE, EMB), F32),
        ],
        compiler_params=pltpu.CompilerParams(vmem_limit_bytes=48 * 1024 * 1024),
    )(*args)


def final_kernel(place, w, *refs):
    *moved, proj_out, pair_out, head_out, emb_out = refs
    total = moved[0][...]
    for block in moved[1:]:
        total = total + block[...].astype(F32)
    emb_out[...] = total
    chan = place[2]
    scale = 1.0 / BINS

    def tile(t):
        at, row = t // TILES * SLOTS + t % TILES // 3, t % 3 * 8
        return w[at, row : row + 8, :] * scale

    proj = [jnp.concatenate([tile(4 * a + b) for b in range(4)], 1) for a in range(4)]
    proj_out[...] = jnp.concatenate(proj, 0)
    for b in range(3):
        for a in range(4):
            t = 16 + (b * 4 + a) * 2
            row = jnp.concatenate([tile(t), tile(t + 1)], 1)
            for k in range(3):
                pair_out[3 * k + b, 8 * a : 8 * a + 8, :] = row[:, CH * k : CH * k + CH]
    row = jnp.concatenate([tile(40), tile(41)], 1)
    for k in range(3):
        line = row[:3, CH * k : CH * k + CH]
        first = jnp.full((3, HALF), chan, jnp.int32) == 0
        head_out[3 * k : 3 * k + 3, :] = jnp.where(first, line[:, :HALF], line[:, HALF:])


def run_final(*args):
    return pl.pallas_call(
        final_kernel,
        out_shape=(
            jax.ShapeDtypeStruct((HALF, EMB), F32),
            jax.ShapeDtypeStruct((9, HALF, CH), F32),
            jax.ShapeDtypeStruct((9, HALF), F32),
            jax.ShapeDtypeStruct((BLOCK, EMB // 2), F32),
        ),
        in_specs=[SMEM] + [VMEM] * (len(args) - 1),
        out_specs=(VMEM,) * 4,
        compiler_params=pltpu.CompilerParams(vmem_limit_bytes=8 * 1024 * 1024),
    )(*args)


def swap(value, axis):
    return lax.ppermute(value, axis, [(0, 1), (1, 0)])


def cycle(value, axes, length, by):
    return lax.ppermute(value, axes, [(i, (i + by) % length) for i in range(length)])


def exchange(value, axes):
    return lax.all_to_all(value, axes, 0, 0, tiled=True)


def local(sizes, embeddings, bin_mask, target, proj_weight, dist_bias, pair_kernel, head_kernel, dilations):
    chips = sizes["yl"] * sizes["x"] * sizes["z"]
    chan = lax.axis_index("chan")
    core = lax.axis_index("core")
    at = (lax.axis_index(GENOME) * 2 + chan) * OWN - HALO
    place = jnp.stack([at, core, chan]).astype(jnp.int32)

    marked, first, rim = run_mark(place, embeddings, bin_mask[None, :], target)
    packed = run_pack(proj_weight.T, dist_bias, pair_kernel, head_kernel)
    other_pack = swap(packed, "chan")
    same = [first, cycle(first, CHIPS, chips, -1), cycle(marked, CHIPS, chips, -2)]
    same += [cycle(same[n], CHIPS, chips, -2) for n in (1, 2)]
    flat = lambda chip, c, h: (chip % chips * 2 + c) * 2 + h
    routes = []
    for i in range(chips):
        routes.append((flat(i, 1, 0), flat(i + 1, 0, 0)))
        routes.append((flat(i, 0, 1), flat(i - AHEAD, 1, 1)))
        routes.append((flat(i, 0, 0), flat(i, 1, 0)))
        routes.append((flat(i, 1, 1), flat(i, 0, 1)))
    rim = lax.ppermute(rim, ALL, routes)
    sibling = [swap(value, "core") for value in same]
    keep, give, w = run_kernel(
        dilations, place, *same, *sibling, rim, packed, other_pack, target
    )

    given = swap(give, "core").astype(F32)
    none = jnp.zeros((1, BLOCK, EMB), F32)
    before = jnp.concatenate([none, given], 0)
    behind = jnp.concatenate([given, none], 0)
    blocks = keep + jnp.where(core == 0, before, behind)
    low, high = blocks[..., : EMB // 2], blocks[..., EMB // 2 :]
    other = swap(jnp.where(chan == 0, high, low).astype(BF16), "chan")
    blocks = jnp.where(chan == 0, low, high) + other.astype(F32)
    moved = [blocks[0]]
    moved += [cycle(blocks[n].astype(BF16), CHIPS, chips, n) for n in range(1, AHEAD)]

    w = exchange(w.reshape(4 * SLOTS, 24, 128), ("core", "chan", "yl", "x"))
    w = jnp.sum(w, axis=0, keepdims=True)
    w = exchange(jnp.broadcast_to(w, (sizes["z"], 24, 128)), "z")
    w = jnp.sum(w, axis=0, keepdims=True)
    w = exchange(jnp.broadcast_to(w, (2 * SLOTS, 24, 128)), ("core", "yl", "x"))
    proj, pair, head, emb = run_final(place, w, *moved)
    return emb, proj.T, pair, head


def solution(mesh):
    split = mesh.devices.reshape(2, 4, 8, 2, 2)
    sizes = dict(yl=2, x=4, z=8, core=2, chan=2)
    fine = Mesh(split, ("yl", "x", "z", "core", "chan"))
    return jax.shard_map(
        functools.partial(local, sizes),
        mesh=fine,
        in_specs=(
            P(GENOME, None),
            P(GENOME),
            P(GENOME, None),
            P(None, "chan"),
            P("chan", None),
            P(None, "chan", None),
            P(None, "chan"),
            P(),
        ),
        out_specs=(P(GENOME, "chan"), P(None, "chan"), P(None, "chan", None), P(None, "chan")),
        check_vma=False,
    )
```

```python
import functools

import jax
import jax.numpy as jnp
from jax import lax
from jax.experimental import pallas as pl
from jax.experimental.pallas import tpu as pltpu
from jax.sharding import Mesh, PartitionSpec as P

F32 = jnp.float32
BF16 = jnp.bfloat16
EMB = 512
CH = 64
HALF = CH // 2
BAND = 256
BINS = 4096
BLOCK = 32
OWN = 16
HALO = 16
ROWS = OWN + 2 * HALO
WIDE = 384
LEAD = 32
PACK = 96
MARKED = EMB + 128
SLOTS = 8
TILES = 21
AHEAD = 5
GENOME = ("yl", "x", "z", "core")
CHIPS = ("yl", "x", "z")
ALL = GENOME + ("chan",)
NT = (((1,), (1,)), ((), ()))
TN = (((0,), (0,)), ((), ()))


def dot(a, b, dims=(((1,), (0,)), ((), ()))):
    return lax.dot_general(a, b, dims, preferred_element_type=F32)


def shift_up(v, by):
    low = lax.broadcasted_iota(jnp.int32, (v.shape[0], 128), 1) < by
    tiles = [pltpu.roll(v[:, t : t + 128], by, 1) for t in range(0, v.shape[1], 128)]
    return jnp.concatenate([jnp.where(low, tiles[n - 1], tiles[n]) for n in range(len(tiles))], 1)


def shift_down(v, by):
    low = lax.broadcasted_iota(jnp.int32, (v.shape[0], 128), 1) < 128 - by
    tiles = [pltpu.roll(v[:, t : t + 128], 128 - by, 1) for t in range(0, v.shape[1], 128)]
    tiles.append(tiles[0])
    return jnp.concatenate(
        [jnp.where(low, tiles[n], tiles[n + 1]) for n in range(len(tiles) - 1)], 1
    )


def silu_and_slope(u, mask):
    t = jnp.tanh(u)
    w = (1.0 + t) * mask
    value = u * w
    return value, w + (value - value * t)


def mark_kernel(place, emb, mask, target, marked, first, rim):
    core = place[1]
    chan = place[2]
    line = jnp.broadcast_to(mask[...].astype(F32), (BLOCK, BLOCK))
    row = lax.broadcasted_iota(jnp.int32, (BLOCK, BLOCK), 0)
    own = jnp.where(row == lax.broadcasted_iota(jnp.int32, (BLOCK, BLOCK), 1), line, 0.0)
    column = jnp.sum(own, axis=1, keepdims=True)
    column = jnp.broadcast_to(column, (BLOCK, 128)).astype(BF16)
    for out in (marked, first):
        out[:, :EMB] = emb[...]
        out[:, EMB:MARKED] = column
    rows = target[pl.ds(pl.multiple_of(24 - 24 * chan, 8), 8), :]
    high = rows.astype(BF16).astype(F32)
    low = rows - high
    high = jnp.concatenate([high[:, :128], high[:, 128:]], 0).astype(BF16)
    low = jnp.concatenate([low[:, :128], low[:, 128:]], 0).astype(BF16)
    first[:OWN, MARKED:] = high
    first[OWN:, MARKED:] = low
    rim[:, :MARKED] = marked[pl.ds(pl.multiple_of(core * OWN, OWN), OWN), :]
    rim[:, MARKED : MARKED + 128] = high
    rim[:, MARKED + 128 :] = low


def pack_kernel(proj, bias, pair, head, packed):
    packed[:HALF, :] = proj[...]
    packed[32:48, :] = jnp.concatenate([bias[:16], bias[16:]], 1)
    taps = [pair[tap].astype(F32) for tap in range(9)]
    packed[48:80, :] = jnp.concatenate(taps[:8], 1).astype(BF16)
    last = jnp.concatenate([taps[8][:16], taps[8][16:]], 1)
    heads = jnp.concatenate([head[...].astype(F32), jnp.zeros((7, HALF), F32)], 0)
    blank = jnp.zeros((16, EMB - 128 - HALF), F32)
    packed[80:96, :] = jnp.concatenate([last, heads, blank], 1).astype(BF16)


def kernel(rates, place, *refs):
    same, sibling = refs[:AHEAD], refs[AHEAD : 2 * AHEAD]
    (
        rim, own_pack, other_pack, target,
        keep_out, give_out, w_out,
        window, wt, bias, kf, kb, hk, hkt,
        ef, mrow, cmask, hz, d0, h1, d1, s1, s1b, sz, aown, q, rgb, tgw, pacc, g1, pg, hg, gs,
    ) = refs[2 * AHEAD :]
    r0 = rates[0]
    r1 = rates[1]
    w0 = place[0]
    core = place[1]
    chan = place[2]
    col = lax.broadcasted_iota(jnp.int32, (1, WIDE), 1)

    def band(r):
        high = jnp.where(w0 + r >= 0, jnp.minimum(r + BAND, BINS - w0), 0)
        return jnp.where((col >= r) & (col < high), 1.0, 0.0).astype(F32)

    window[...] = jnp.zeros_like(window)
    for n in range(AHEAD):
        at = LEAD + 64 * n + HALO - OWN * chan
        window[pl.ds(pl.multiple_of(at, 16), BLOCK), :] = same[n][:, :MARKED]
        at = at + BLOCK * (1 - 2 * core)
        window[pl.ds(pl.multiple_of(at, 16), BLOCK), :] = sibling[n][:, :MARKED]

    @pl.when((core == 0) & (chan == 0))
    def _():
        window[LEAD : LEAD + OWN, :] = rim[:, :MARKED]

    @pl.when((core == 1) & (chan == 1))
    def _():
        window[LEAD + 288 : LEAD + 304, :] = rim[:, :MARKED]

    win = window.at[LEAD : LEAD + WIDE]

    flip = jnp.full((PACK, EMB), chan, jnp.int32) == 0
    mine, other = own_pack[...].astype(F32), other_pack[...].astype(F32)
    halves = [jnp.where(flip, mine, other), jnp.where(flip, other, mine)]
    wt[...] = jnp.concatenate([h[:HALF] for h in halves], 0)
    rows = []
    for h in halves:
        rows += [h[32:48, :BAND], h[32:48, BAND:]]
    bias[...] = jnp.concatenate(
        [0.5 * jnp.concatenate(rows, 0), jnp.zeros((CH, WIDE - BAND), F32)], 1
    )
    taps = []
    for tap in range(9):
        parts = []
        for h in halves:
            if tap < 8:
                parts.append(h[48:80, tap * CH : tap * CH + CH])
            else:
                parts += [h[80:96, :CH], h[80:96, CH : 2 * CH]]
        taps.append(jnp.concatenate(parts, 0))
    grid = lambda pick: jnp.concatenate(
        [jnp.concatenate([taps[pick(n, m)] for m in range(3)], 1) for n in range(3)], 0
    )
    kf[...] = (0.5 * grid(lambda b, a: 3 * a + b)).astype(BF16)
    kb[...] = (0.5 * grid(lambda a, b: 3 * a + b)).T.astype(BF16)
    heads = jnp.concatenate([h[80:96, 128 : 128 + HALF] for h in halves], 1)
    rest = jnp.zeros((5, CH), F32)
    rows = []
    for b in range(3):
        rows += [heads[3 * a + b : 3 * a + b + 1] for a in range(3)] + [rest]
    hk[...] = jnp.concatenate(rows, 0).astype(BF16)
    rows = []
    for a in range(3):
        rows += [heads[3 * a : 3 * a + 3], rest] * 2
    hkt[...] = (0.5 * jnp.concatenate(rows, 0)).T.astype(BF16)

    wide = win[:, :EMB].astype(F32)
    ef[...] = wide[:ROWS]
    marks = win[:, EMB:].astype(F32)
    mrow[...] = marks[:ROWS]
    cmask[...] = marks.T[:8]

    def joined(parts):
        whole = parts[0].astype(F32) + parts[1].astype(F32)
        return jnp.concatenate([whole[:8], whole[8:]], 1)

    def sent(ref):
        return joined([ref[:OWN, MARKED:], ref[OWN:, MARKED:]])

    def at_core(zero, one):
        return jnp.where(jnp.full((8, BAND), core, jnp.int32) == 0, zero, one)

    before = joined([rim[:, MARKED : MARKED + 128], rim[:, MARKED + 128 :]])
    before = at_core(before, sent(sibling[0]))
    behind = at_core(sent(sibling[0]), sent(sibling[1]))
    tgt = jnp.where(
        jnp.full((BLOCK, BAND), chan, jnp.int32) == 0,
        jnp.concatenate([before, target[:24]], 0),
        jnp.concatenate([target[8:], behind], 0),
    )
    padded = jnp.concatenate([tgt, jnp.zeros((BLOCK, WIDE - BAND), F32)], 1)
    tgw[...] = pltpu.roll(padded, 8, 1, stride=1, stride_axis=0)

    for b in range(ROWS // 8):
        e8 = ef[b * 8 : b * 8 + 8, :]
        w = 0.5 * wt[...]
        a = jnp.concatenate([(w * e8[k : k + 1]).astype(BF16) for k in range(8)], 0)
        if 2 <= b < 4:
            aown[(b - 2) * 512 : (b - 1) * 512, :] = a
        p = dot(a, win[:, :EMB], NT)
        for k in range(8):
            r = b * 8 + k
            u = p[k * CH : k * CH + CH, :] + shift_up(bias[...], r)
            value, gain = silu_and_slope(u, band(r))
            hz[r] = value.astype(BF16)
            d0[r] = gain

    def near(field, r, step):
        return jnp.concatenate([field[r - step], field[r], field[r + step]], 0)

    def side(rows):
        return jnp.concatenate(rows, 1)

    def part(v, k):
        return v[:, k * WIDE : k * WIDE + WIDE]

    def second(n, _):
        first = 4 + n * 20
        p = dot(kf[...], side([near(hz, first + k, r0) for k in range(20)]))
        ones = []
        for k in range(20):
            r = first + k
            pk = part(p, k)
            u = shift_up(pk[:CH], r0) + pk[CH : 2 * CH] + shift_down(pk[2 * CH :], r0)
            value, gain = silu_and_slope(u, band(r))
            ones.append(value.astype(BF16))
            h1[r] = ones[k]
            d1[r] = gain
        p = dot(hk[...], side(ones))
        for k in range(20):
            pk = part(p, k)
            q[first + k] = shift_up(pk[:8], r1) + pk[8:16] + shift_down(pk[16:24], r1)
        return 0

    lax.fori_loop(0, 2, second, 0)

    which = lax.broadcasted_iota(jnp.int32, (8, WIDE), 0)

    def residual(n, _):
        for k in range(16):
            r = 8 + n * 16 + k
            pred = q[r - r1][0:1] + q[r][1:2] + q[r + r1][2:3]
            mark = mrow[pl.ds(r, 1), :]
            lm = jnp.concatenate([mark] * (WIDE // 128), 1) * cmask[0:1] * band(r)
            rg = lm * (pred - tgw[pl.ds(r - 8, 1), :]) * (1.0 / BAND)
            rg = jnp.broadcast_to(rg, (8, WIDE))
            taps = jnp.where(
                which == 0,
                shift_down(rg, r1),
                jnp.where(which == 1, rg, jnp.where(which == 2, shift_up(rg, r1), 0.0)),
            )
            high = taps.astype(BF16).astype(F32)
            rgb[r] = jnp.concatenate([high, taps - high], 0).astype(BF16)
        return 0

    lax.fori_loop(0, 2, residual, 0)

    def slope(n, _):
        first = 12 + n * 24
        h = dot(hkt[...], side([near(rgb, first + k, -r1) for k in range(24)]))
        for k in range(24):
            r = first + k
            sf = part(h, k) * d1[r]
            s = sf.astype(BF16)
            s1[r] = s
            sf = s.astype(F32)
            s1b[r] = jnp.concatenate(
                [shift_down(sf, r0).astype(BF16), s, shift_up(sf, r0).astype(BF16)], 0
            )
        return 0

    lax.fori_loop(0, 1, slope, 0)

    rows = range(HALO, HALO + OWN)
    pg[...] = dot(side([s1b[r] for r in rows]), side([near(hz, r, r0) for r in rows]), NT)
    hg[...] = dot(side([rgb[r] for r in rows]), side([near(h1, r, r1) for r in rows]), NT)
    p = dot(kb[...], side([near(s1, r, -r0) for r in rows]))
    for k, r in enumerate(rows):
        pk = part(p, k)
        zg = shift_down(pk[:CH], r0) + pk[CH : 2 * CH] + shift_up(pk[2 * CH :], r0)
        sz[k * CH : k * CH + CH, :] = (zg * d0[r]).astype(BF16)

    pacc[...] = jnp.zeros_like(pacc)

    w = wt[...]
    for n in range(4):
        t = dot(sz[n * 256 : n * 256 + 256, :], win[:, :EMB])
        for k in range(4):
            i = n * 4 + k
            tr = t[k * CH : (k + 1) * CH]
            g1[i : i + 1, :] = jnp.sum(w * tr, axis=0, keepdims=True)
            pacc[...] += tr * ef[HALO + i : HALO + i + 1, :]
    g = dot(sz[...], aown[...], TN)
    g = 2.0 * g
    gs[...] = g
    gs[HALO : HALO + OWN, :] = g[HALO : HALO + OWN] + g1[...]
    for n in range(2 * AHEAD - 1):
        block = gs[pl.ds(pl.multiple_of(BLOCK * n + HALO - OWN * chan, 16), BLOCK), :]
        if n % 2:
            give_out[n // 2] = block.astype(BF16)
        else:
            keep_out[n // 2] = block

    heads = hg[0:8] + hg[8:16]
    blank = jnp.zeros((8, 256 - 3 * CH), F32)
    for half in range(2):
        tiles = []
        for a in range(4):
            for b in range(4):
                tiles.append(pacc[half * 32 + a * 8 : half * 32 + a * 8 + 8, b * 128 : b * 128 + 128])
        for b in range(3):
            for a in range(4):
                at = b * CH + half * 32 + a * 8
                row = jnp.concatenate([pg[at : at + 8, :], blank], 1)
                tiles += [row[:, :128], row[:, 128:]]
        row = jnp.concatenate([heads, blank], 1)
        tiles += [row[:, :128], row[:, 128:]]
        for t, tile in enumerate(tiles):
            at, row = half * SLOTS + t % TILES // 3, t % 3 * 8
            w_out[t // TILES, at, row : row + 8, :] = tile
        for t in range(2):
            w_out[t, half * SLOTS + SLOTS - 1] = jnp.zeros((24, 128), F32)


VMEM = pl.BlockSpec(memory_space=pltpu.VMEM)
SMEM = pl.BlockSpec(memory_space=pltpu.SMEM)


def run_mark(place, *args):
    return pl.pallas_call(
        mark_kernel,
        out_shape=(
            jax.ShapeDtypeStruct((BLOCK, MARKED), BF16),
            jax.ShapeDtypeStruct((BLOCK, MARKED + 128), BF16),
            jax.ShapeDtypeStruct((OWN, MARKED + 256), BF16),
        ),
        in_specs=[SMEM] + [VMEM] * len(args),
        out_specs=(VMEM,) * 3,
        compiler_params=pltpu.CompilerParams(vmem_limit_bytes=8 * 1024 * 1024),
    )(place, *args)


def run_pack(*args):
    return pl.pallas_call(
        pack_kernel,
        out_shape=jax.ShapeDtypeStruct((PACK, EMB), BF16),
        in_specs=[VMEM] * len(args),
        out_specs=VMEM,
        compiler_params=pltpu.CompilerParams(vmem_limit_bytes=8 * 1024 * 1024),
    )(*args)


def run_kernel(*args):
    return pl.pallas_call(
        kernel,
        out_shape=(
            jax.ShapeDtypeStruct((AHEAD, BLOCK, EMB), F32),
            jax.ShapeDtypeStruct((AHEAD - 1, BLOCK, EMB), BF16),
            jax.ShapeDtypeStruct((2, 2 * SLOTS, 24, 128), F32),
        ),
        in_specs=[SMEM] * 2 + [VMEM] * (len(args) - 2),
        out_specs=(VMEM, VMEM, VMEM),
        scratch_shapes=[
            pltpu.VMEM((LEAD + WIDE, MARKED), BF16),
            pltpu.VMEM((CH, EMB), F32),
            pltpu.VMEM((CH, WIDE), F32),
            pltpu.VMEM((3 * CH, 3 * CH), BF16),
            pltpu.VMEM((3 * CH, 3 * CH), BF16),
            pltpu.VMEM((24, CH), BF16),
            pltpu.VMEM((CH, 48), BF16),
            pltpu.VMEM((ROWS, EMB), F32),
            pltpu.VMEM((ROWS, 128), F32),
            pltpu.VMEM((8, WIDE), F32),
            pltpu.VMEM((ROWS, CH, WIDE), BF16),
            pltpu.VMEM((ROWS, CH, WIDE), F32),
            pltpu.VMEM((ROWS, CH, WIDE), BF16),
            pltpu.VMEM((ROWS, CH, WIDE), F32),
            pltpu.VMEM((ROWS, CH, WIDE), BF16),
            pltpu.VMEM((ROWS, 3 * CH, WIDE), BF16),
            pltpu.VMEM((OWN * CH, WIDE), BF16),
            pltpu.VMEM((OWN * CH, EMB), BF16),
            pltpu.VMEM((ROWS, 8, WIDE), F32),
            pltpu.VMEM((ROWS, 16, WIDE), BF16),
            pltpu.VMEM((BLOCK, WIDE), F32),
            pltpu.VMEM((CH, EMB), F32),
            pltpu.VMEM((OWN, EMB), F32),
            pltpu.VMEM((3 * CH, 3 * CH), F32),
            pltpu.VMEM((16, 3 * CH), F32),
            pltpu.VMEM((WIDE, EMB), F32),
        ],
        compiler_params=pltpu.CompilerParams(vmem_limit_bytes=48 * 1024 * 1024),
    )(*args)


def final_kernel(place, w, *refs):
    *moved, proj_out, pair_out, head_out, emb_out = refs
    total = moved[0][...]
    for block in moved[1:]:
        total = total + block[...].astype(F32)
    emb_out[...] = total
    chan = place[2]
    scale = 1.0 / BINS

    def tile(t):
        at, row = t // TILES * SLOTS + t % TILES // 3, t % 3 * 8
        return w[at, row : row + 8, :] * scale

    proj = [jnp.concatenate([tile(4 * a + b) for b in range(4)], 1) for a in range(4)]
    proj_out[...] = jnp.concatenate(proj, 0)
    for b in range(3):
        for a in range(4):
            t = 16 + (b * 4 + a) * 2
            row = jnp.concatenate([tile(t), tile(t + 1)], 1)
            for k in range(3):
                pair_out[3 * k + b, 8 * a : 8 * a + 8, :] = row[:, CH * k : CH * k + CH]
    row = jnp.concatenate([tile(40), tile(41)], 1)
    for k in range(3):
        line = row[:3, CH * k : CH * k + CH]
        first = jnp.full((3, HALF), chan, jnp.int32) == 0
        head_out[3 * k : 3 * k + 3, :] = jnp.where(first, line[:, :HALF], line[:, HALF:])


def run_final(*args):
    return pl.pallas_call(
        final_kernel,
        out_shape=(
            jax.ShapeDtypeStruct((HALF, EMB), F32),
            jax.ShapeDtypeStruct((9, HALF, CH), F32),
            jax.ShapeDtypeStruct((9, HALF), F32),
            jax.ShapeDtypeStruct((BLOCK, EMB // 2), F32),
        ),
        in_specs=[SMEM] + [VMEM] * (len(args) - 1),
        out_specs=(VMEM,) * 4,
        compiler_params=pltpu.CompilerParams(vmem_limit_bytes=8 * 1024 * 1024),
    )(*args)


def swap(value, axis):
    return lax.ppermute(value, axis, [(0, 1), (1, 0)])


def cycle(value, axes, length, by):
    return lax.ppermute(value, axes, [(i, (i + by) % length) for i in range(length)])


def exchange(value, axes):
    return lax.all_to_all(value, axes, 0, 0, tiled=True)


def local(sizes, embeddings, bin_mask, target, proj_weight, dist_bias, pair_kernel, head_kernel, dilations):
    chips = sizes["yl"] * sizes["x"] * sizes["z"]
    chan = lax.axis_index("chan")
    core = lax.axis_index("core")
    at = (lax.axis_index(GENOME) * 2 + chan) * OWN - HALO
    place = jnp.stack([at, core, chan]).astype(jnp.int32)

    marked, first, rim = run_mark(place, embeddings, bin_mask[None, :], target)
    packed = run_pack(proj_weight.T, dist_bias, pair_kernel, head_kernel)
    other_pack = swap(packed, "chan")
    same = [first, cycle(first, CHIPS, chips, -1), cycle(marked, CHIPS, chips, -2)]
    same += [cycle(same[n], CHIPS, chips, -2) for n in (1, 2)]
    flat = lambda chip, c, h: (chip % chips * 2 + c) * 2 + h
    routes = []
    for i in range(chips):
        for c in range(2):
            routes.append((flat(i, c, 0), flat(i + 1, c, 0)))
            routes.append((flat(i, c, 1), flat(i - AHEAD, c, 1)))
    rim = swap(lax.ppermute(rim, ALL, routes), "core")
    sibling = [swap(value, "core") for value in same]
    keep, give, w = run_kernel(
        dilations, place, *same, *sibling, rim, packed, other_pack, target
    )

    given = swap(give, "core").astype(F32)
    none = jnp.zeros((1, BLOCK, EMB), F32)
    before = jnp.concatenate([none, given], 0)
    behind = jnp.concatenate([given, none], 0)
    blocks = keep + jnp.where(core == 0, before, behind)
    low, high = blocks[..., : EMB // 2], blocks[..., EMB // 2 :]
    other = swap(jnp.where(chan == 0, high, low).astype(BF16), "chan")
    blocks = jnp.where(chan == 0, low, high) + other.astype(F32)
    moved = [blocks[0]]
    moved += [cycle(blocks[n].astype(BF16), CHIPS, chips, n) for n in range(1, AHEAD)]

    w = exchange(w.reshape(4 * SLOTS, 24, 128), ("core", "chan", "yl", "x"))
    w = jnp.sum(w, axis=0, keepdims=True)
    w = exchange(jnp.broadcast_to(w, (sizes["z"], 24, 128)), "z")
    w = jnp.sum(w, axis=0, keepdims=True)
    w = exchange(jnp.broadcast_to(w, (2 * SLOTS, 24, 128)), ("core", "yl", "x"))
    proj, pair, head, emb = run_final(place, w, *moved)
    return emb, proj.T, pair, head


def solution(mesh):
    split = mesh.devices.reshape(2, 4, 8, 2, 2)
    sizes = dict(yl=2, x=4, z=8, core=2, chan=2)
    fine = Mesh(split, ("yl", "x", "z", "core", "chan"))
    return jax.shard_map(
        functools.partial(local, sizes),
        mesh=fine,
        in_specs=(
            P(GENOME, None),
            P(GENOME),
            P(GENOME, None),
            P(None, "chan"),
            P("chan", None),
            P(None, "chan", None),
            P(None, "chan"),
            P(),
        ),
        out_specs=(P(GENOME, "chan"), P(None, "chan"), P(None, "chan", None), P(None, "chan")),
        check_vma=False,
    )
```
